32 devices in a mesh: dp: 4 (over y, x), ctx: 8 (over z, core).
Axes of the slice: x: 2, y: 2, z: 4, core: 2. Of those that a mesh axis runs over, the one named last changes fastest.
Arguments:
- query_rows: bfloat16 [4, 1024, 2048], P('dp', 'ctx'), may hold values from -6 to 6
- key_rows: bfloat16 [4, 1024, 512], P('dp', 'ctx'), may hold values from -6 to 6
- value_rows: bfloat16 [4, 1024, 512], P('dp', 'ctx'), may hold values from -6 to 6
- out_grad: bfloat16 [4, 1024, 2048], P('dp', 'ctx'), may hold values from -6 to 6
- segment_ids: int32 [4, 1024], P('dp', 'ctx'), may hold values from 0 to 7, never falling along the last dimension, each value on 1 to 256 neighbouring positions
- home_rows: int32 [4, 128], P('dp', 'ctx'), may hold values from 0 to 3, as said below
Outputs:
- routed: bfloat16 [4, 8, 4, 8, 8, 2048], P('dp', 'ctx')
- query_grad: bfloat16 [4, 1024, 2048], P('dp', 'ctx')
- key_grad: bfloat16 [4, 1024, 512], P('dp', 'ctx')
- value_grad: bfloat16 [4, 1024, 512], P('dp', 'ctx')
The draws below stay inside these ranges and needn't reach their ends.
Inputs may be any that keep to these rules, and one draw needn't show every extreme that they name: `segment_ids`: ids never fall along a sequence; every document holds 1 to 256 tokens, and some document holds exactly 256. `home_rows`: among the 16 stretches of one block, at most 8 name the same dp row; in every block column some dp row is named by exactly 8 stretches of every dp row's block.
All inputs are finite; a program needn't handle non-finite values.
Results may differ from the reference program's by a relative error of at most 0.014.
Values may be sent and summed in bfloat16 or wider, within the bound.
No kernel may reach another device: no remote copies, remote signals or barrier semaphores. Data moves between devices by JAX's collectives and lax.ppermute only.
A program may use at most 64 MiB of HBM per device.

```python
import math
import jax
import jax.numpy as jnp
import numpy as np
from jax import lax

HEAD_DIM = 128
QHEADS = 16
KVHEADS = 4
BLOCK_TOK = 128
SPAN = 2
STRETCH = 8
GROUP = 4
STRETCHES = 16
SEQS = 4
BLOCKS = 8
LENGTH = 1024
MAXDOC = 256
DOCS = 8
CAPACITY = 8


def draw_query_rows(key, part):
    width = QHEADS * HEAD_DIM
    field = jnp.clip(jax.random.normal(jax.random.fold_in(key, 21), (SEQS, LENGTH, width)), -6.0, 6.0)
    return field.astype(jnp.bfloat16)


def draw_key_rows(key, part):
    width = KVHEADS * HEAD_DIM
    field = jnp.clip(jax.random.normal(jax.random.fold_in(key, 31), (SEQS, LENGTH, width)), -6.0, 6.0)
    return field.astype(jnp.bfloat16)


def draw_home_rows(key, part):
    full_rows = jax.random.randint(jax.random.fold_in(key, 12), (BLOCKS,), 0, SEQS).astype(jnp.int32)
    block_keys = jax.random.split(jax.random.fold_in(key, 11), SEQS * BLOCKS)
    targets = jnp.tile(full_rows, SEQS)

    def one_block(sub_key, target):
        key_one, key_two = jax.random.split(sub_key)
        spread = (target + 1 + jnp.arange((SEQS - 1) * CAPACITY, dtype=jnp.int32) // CAPACITY) % SEQS
        chosen = jax.random.permutation(key_one, spread)[:STRETCHES - CAPACITY]
        filled = jnp.concatenate([target + jnp.zeros((CAPACITY,), jnp.int32), chosen.astype(jnp.int32)])
        return jax.random.permutation(key_two, filled)
    return jax.vmap(one_block)(block_keys, targets).reshape(SEQS, BLOCKS * STRETCHES).astype(jnp.int32)


def block_levels(stream_key, shape, cuts, low, largest):
    gain = 1.0
    for position, parts in cuts:
        draws = jax.random.uniform(jax.random.fold_in(jax.random.fold_in(stream_key, 6), position), (parts,), jnp.float32, low / len(cuts), largest / len(cuts))
        gain = gain * jnp.repeat(jnp.exp(draws), shape[position] // parts).reshape((-1,) + (1,) * (len(shape) - 1 - position))
    return gain


def split_up(count, total, bound, slope):
    portions = [(1 << 20) // math.isqrt(standing ** slope) + 1 for standing in range(2, count + 1)]
    surplus, counts = total - bound - (count - 1), [1] * (count - 1)
    while surplus > 0:
        free = [i for i in range(count - 1) if counts[i] < bound]
        pool, remaining = sum([portions[i] for i in free]), surplus
        for i in free:
            extra = min(bound - counts[i], max(1, remaining * portions[i] // pool), surplus)
            counts[i] = counts[i] + extra
            surplus = surplus - extra
    return np.array([bound] + counts)


def uneven_parts(rng, count, total, bound, lean):
    if count == 2:
        one = jax.random.randint(rng, (), max(1, total - bound), min(bound, total - 1) + 1)
        return jnp.stack([one, total - one])
    tallies = jnp.asarray(split_up(count, total, bound, lean), jnp.int32)
    twos = (count - 1) // 2
    donor, sink = tallies[1:1 + 2 * twos:2], tallies[2:2 + 2 * twos:2]
    slack = jnp.minimum(donor - 1, bound - sink)
    moved = jax.random.randint(jax.random.fold_in(rng, 1), (twos,), 0, 1 << 20) % (slack + 1)
    tallies = tallies.at[1:1 + 2 * twos:2].set(donor - moved).at[2:2 + 2 * twos:2].set(sink + moved)
    return tallies[jax.random.permutation(jax.random.fold_in(rng, 2), count)]


def noise(own_key, extent, scale, limit, pieces=(), kind=jnp.bfloat16):
    values = jax.random.normal(own_key, extent, jnp.float32) * scale
    if len(pieces) > 0:
        values = block_levels(own_key, extent, pieces, -0.22, 0.18) * values
    return jnp.clip(values, min=-limit, max=limit).astype(kind)


def setup_inputs(seed: int = 0) -> dict:
    key_list = jax.random.split(jax.random.key(seed), 7)
    return {
        "query_rows": draw_query_rows(jax.random.fold_in(key_list[6], 71), 0),
        "key_rows": draw_key_rows(jax.random.fold_in(key_list[6], 71), 0),
        "value_rows": noise(key_list[2], (SEQS, LENGTH, KVHEADS * HEAD_DIM), 1.0, 6.0, ((0, 4), (1, 8))),
        "out_grad": noise(key_list[3], (SEQS, LENGTH, QHEADS * HEAD_DIM), 1.0, 6.0, ((0, 4), (1, 8))),
        "segment_ids": jax.vmap(lambda own: jnp.searchsorted(jnp.cumsum(uneven_parts(own, DOCS, LENGTH, MAXDOC, 2)), jnp.arange(LENGTH), side="right"))(jax.random.split(key_list[4], SEQS)).reshape((SEQS, LENGTH)).astype(jnp.int32),
        "home_rows": draw_home_rows(jax.random.fold_in(key_list[6], 71), 0),
    }


def block_terms(query_block, key_window, value_window, grad_block, allowed):
    scaling = 1.0 / math.sqrt(HEAD_DIM)
    window = key_window.shape[0]
    query_heads = query_block.astype(jnp.float32).reshape(BLOCK_TOK, KVHEADS, GROUP, HEAD_DIM)
    key_heads = key_window.astype(jnp.float32).reshape(window, KVHEADS, HEAD_DIM)
    value_heads = value_window.astype(jnp.float32).reshape(window, KVHEADS, HEAD_DIM)
    grad_heads = grad_block.astype(jnp.float32).reshape(BLOCK_TOK, KVHEADS, GROUP, HEAD_DIM)
    scores = jnp.einsum('qkgd,nkd->kgqn', query_heads, key_heads) * scaling
    scores = jnp.where(allowed, scores, -jnp.inf)
    highest = lax.optimization_barrier(jnp.max(scores, axis=-1, keepdims=True))
    exp_total = lax.optimization_barrier(jnp.sum(jnp.exp(scores - highest), axis=-1, keepdims=True))
    log_total = highest + jnp.log(exp_total)
    weights = jnp.exp(scores - log_total)
    weights_low = lax.optimization_barrier(weights.astype(jnp.bfloat16)).astype(jnp.float32)
    attended = jnp.einsum('kgqn,nkd->qkgd', weights_low, value_heads)
    attended = attended.reshape(BLOCK_TOK, QHEADS * HEAD_DIM).astype(jnp.bfloat16)
    attended_heads = lax.optimization_barrier(attended).astype(jnp.float32).reshape(BLOCK_TOK, KVHEADS, GROUP, HEAD_DIM)
    row_delta = jnp.einsum('qkgd,qkgd->kgq', grad_heads, attended_heads)
    grad_weights = jnp.einsum('qkgd,nkd->kgqn', grad_heads, value_heads)
    grad_scores = (weights * (grad_weights - row_delta[..., None]) * scaling).astype(jnp.bfloat16)
    grad_scores = lax.optimization_barrier(grad_scores).astype(jnp.float32)
    query_grad = jnp.einsum('kgqn,nkd->qkgd', grad_scores, key_heads)
    query_grad = query_grad.reshape(BLOCK_TOK, QHEADS * HEAD_DIM).astype(jnp.bfloat16)
    key_terms = jnp.einsum('kgqn,qkgd->nkd', grad_scores, query_heads).reshape(window, KVHEADS * HEAD_DIM)
    value_terms = jnp.einsum('kgqn,qkgd->nkd', weights_low, grad_heads).reshape(window, KVHEADS * HEAD_DIM)
    return (attended, query_grad, key_terms, value_terms)

def reference(query_rows, key_rows, value_rows, out_grad, segment_ids, home_rows):
    padding = SPAN * BLOCK_TOK
    window = (SPAN + 1) * BLOCK_TOK
    kv_width = KVHEADS * HEAD_DIM
    q_width = QHEADS * HEAD_DIM

    def one_sequence(items):
        queries, key_seq, value_seq, grad_seq, seg_seq = items
        key_pad = jnp.concatenate([jnp.zeros((padding, kv_width), jnp.bfloat16), key_seq], axis=0)
        value_pad = jnp.concatenate([jnp.zeros((padding, kv_width), jnp.bfloat16), value_seq], axis=0)
        seg_pad = jnp.concatenate([jnp.full((padding,), -1, jnp.int32), seg_seq], axis=0)

        def visit(carry, index):
            key_acc, value_acc = carry
            start = (index * BLOCK_TOK).astype(jnp.int32)
            query_block = lax.dynamic_slice_in_dim(queries, start, BLOCK_TOK, 0)
            grad_block = lax.dynamic_slice_in_dim(grad_seq, start, BLOCK_TOK, 0)
            seg_query = lax.dynamic_slice_in_dim(seg_seq, start, BLOCK_TOK, 0)
            key_window = lax.dynamic_slice_in_dim(key_pad, start, window, 0)
            value_window = lax.dynamic_slice_in_dim(value_pad, start, window, 0)
            seg_key = lax.dynamic_slice_in_dim(seg_pad, start, window, 0)
            pos_query = start + jnp.arange(BLOCK_TOK, dtype=jnp.int32)
            pos_key = start - padding + jnp.arange(window, dtype=jnp.int32)
            allowed = (seg_query[:, None] == seg_key[None, :]) & (pos_key[None, :] <= pos_query[:, None]) & (pos_key[None, :] >= 0)
            attended, query_grad, key_terms, value_terms = block_terms(query_block, key_window, value_window, grad_block, allowed)
            key_acc = lax.dynamic_update_slice_in_dim(key_acc, lax.dynamic_slice_in_dim(key_acc, start, window, 0) + key_terms, start, 0)
            value_acc = lax.dynamic_update_slice_in_dim(value_acc, lax.dynamic_slice_in_dim(value_acc, start, window, 0) + value_terms, start, 0)
            return ((key_acc, value_acc), (attended, query_grad))
        zero_acc = jnp.zeros((padding + LENGTH, kv_width), jnp.float32)
        (key_acc, value_acc), (attended, query_grad) = lax.scan(visit, (zero_acc, zero_acc), jnp.arange(BLOCKS, dtype=jnp.int32))
        return (attended.reshape(LENGTH, q_width), query_grad.reshape(LENGTH, q_width), key_acc[padding:].astype(jnp.bfloat16), value_acc[padding:].astype(jnp.bfloat16))
    attended, query_grad, key_grad, value_grad = lax.map(one_sequence, (query_rows, key_rows, value_rows, out_grad, segment_ids))
    stretch_rows = attended.reshape(SEQS, BLOCKS, STRETCHES, STRETCH * q_width).astype(jnp.float32)
    home_ids = home_rows.reshape(SEQS, BLOCKS, STRETCHES)
    positions = jnp.arange(STRETCHES, dtype=jnp.int32)
    matching = (home_ids[..., :, None] == home_ids[..., None, :]) & (positions[None, :] < positions[:, None])
    slot_index = lax.optimization_barrier(jnp.sum(matching.astype(jnp.int32), axis=-1))

    def to_home(target):
        select = ((home_ids == target)[..., None, :] & (slot_index[..., None, :] == jnp.arange(CAPACITY, dtype=jnp.int32)[:, None])).astype(jnp.float32)
        return jnp.einsum('scjk,sckx->csjx', select, stretch_rows).astype(jnp.bfloat16)
    routed = lax.map(to_home, jnp.arange(SEQS, dtype=jnp.int32))
    routed = routed.reshape(SEQS, BLOCKS, SEQS, CAPACITY, STRETCH, q_width)
    return (routed, query_grad, key_grad, value_grad)
```

```python
import functools
import math

import jax
import jax.numpy as jnp
from jax import lax
from jax.experimental import pallas as pl
from jax.experimental.pallas import tpu as pltpu
from jax.sharding import PartitionSpec as P

HEAD_DIM = 128
GROUP = 4
SEG_ROWS = 16
F32 = jnp.float32
BF16 = jnp.bfloat16
NEG = -1e30

NT = (((1,), (1,)), ((), ()))
NN = (((1,), (0,)), ((), ()))
TN = (((0,), (0,)), ((), ()))


def dot(a, b, dims):
    return lax.dot_general(a, b, dims, preferred_element_type=F32)


def stacked(ref, g):
    heads = [
        ref[:, (g * GROUP + h) * HEAD_DIM : (g * GROUP + h + 1) * HEAD_DIM] for h in range(GROUP)
    ]
    return jnp.concatenate(heads, axis=0)


def window(g, block, own_ref, r_ref, near):
    cols = slice(g * HEAD_DIM, (g + 1) * HEAD_DIM)
    keys = (own_ref[0:block, cols], near[0:block, cols], r_ref[0:block, cols])
    values = (
        own_ref[block : 2 * block, cols],
        near[block : 2 * block, cols],
        r_ref[block : 2 * block, cols],
    )
    return keys, values


def near_block(column, b_ref, c_ref):
    return jnp.where(lax.rem(column, 2) == 0, c_ref[...], b_ref[...])


def triangle(block, copies):
    key_pos = lax.broadcasted_iota(jnp.int32, (block, copies * block), 0)
    query_pos = lax.broadcasted_iota(jnp.int32, (block, copies * block), 1)
    return key_pos <= lax.rem(query_pos, block)


def repartner(index, k, count):
    if count & (count - 1) == 0:
        return index ^ k
    return lax.rem(index + k, count)


def fwd_kernel(n_dp, capacity, info_ref, home_ref, q_ref, own_ref, r_ref, b_ref, c_ref, *rest):
    p_ref = rest[0]
    sends = rest[1 : 1 + n_dp]
    packed, counts, sems = rest[1 + n_dp :]
    block = q_ref.shape[0]
    column, row = info_ref[0], info_ref[1]
    pieces = home_ref.shape[0]
    piece_len = block // pieces
    packed[...] = jnp.zeros_like(packed)
    near = near_block(column, b_ref, c_ref)

    def seg_of(value):
        return value[2 * block : 2 * block + SEG_ROWS, 0:block].astype(F32)[0:1]

    seg_own, seg_near, seg_far = seg_of(own_ref), seg_of(near), seg_of(r_ref)
    first = seg_own[:, 0:1]
    reach = jnp.where(column >= 1, jnp.sum((seg_near == first).astype(F32), axis=1, keepdims=True), 0.0)
    reach = reach + jnp.where(
        column >= 2, jnp.sum((seg_far == first).astype(F32), axis=1, keepdims=True), 0.0
    )
    key_pos = lax.broadcasted_iota(jnp.int32, (block, block), 0).astype(F32)
    tri = triangle(block, 1)
    seg_rows = jnp.broadcast_to(seg_own, (block, block))
    joined = seg_rows == first
    own_ok = seg_rows == seg_rows.T
    far_ok = (key_pos >= 2 * block - reach) & joined
    near_ok = (key_pos >= block - reach) & joined
    bias_x = jnp.where((tri & own_ok) | (~tri & far_ok), 0.0, NEG)
    bias_n = jnp.where(near_ok, 0.0, NEG)
    bias_x = jnp.concatenate([bias_x] * GROUP, axis=1)
    bias_n = jnp.concatenate([bias_n] * GROUP, axis=1)
    tri_g = triangle(block, GROUP)
    scaling = math.log2(math.e) / math.sqrt(HEAD_DIM)

    for d in range(n_dp):
        counts[d] = 0
    place = []
    for m in range(pieces):
        home = home_ref[m]
        slot = counts[home]
        counts[home] = slot + 1
        place.append(((home ^ row) if n_dp & (n_dp - 1) == 0 else lax.rem(home - row + n_dp, n_dp), slot))

    for g in range(own_ref.shape[1] // HEAD_DIM):
        keys, values = window(g, block, own_ref, r_ref, near)
        queries = stacked(q_ref, g)
        s_x = jnp.where(tri_g, dot(keys[0], queries, NT), dot(keys[2], queries, NT))
        s_x = s_x * scaling + bias_x
        s_n = dot(keys[1], queries, NT) * scaling + bias_n
        highest = jnp.max(jnp.maximum(s_x, s_n), axis=0, keepdims=True)
        e_x = jnp.exp2(s_x - highest)
        e_n = jnp.exp2(s_n - highest)
        inverse = 1.0 / jnp.sum(e_x + e_n, axis=0, keepdims=True)
        w_x = e_x * inverse
        w_n = (e_n * inverse).astype(BF16)
        p_ref[g, 0:block] = w_x.astype(BF16)
        p_ref[g, block : 2 * block] = w_n
        w_0 = jnp.where(tri_g, w_x, 0.0).astype(BF16)
        w_2 = jnp.where(tri_g, 0.0, w_x).astype(BF16)
        weights = jnp.concatenate([w_0, w_n, w_2], axis=0)
        attended = dot(weights, jnp.concatenate(values, axis=0), TN)
        for h in range(GROUP):
            cols = slice((g * GROUP + h) * HEAD_DIM, (g * GROUP + h + 1) * HEAD_DIM)
            tile = attended[h * block : (h + 1) * block].reshape(pieces, piece_len, HEAD_DIM)
            for m in range(pieces):
                packed[place[m][0], place[m][1], :, cols] = tile[m].astype(BF16)
    copies = [pltpu.make_async_copy(packed.at[k], sends[k], sems.at[k]) for k in range(n_dp)]
    for copy in copies:
        copy.start()
    for copy in copies:
        copy.wait()


def bwd_kernel(info_ref, q_ref, do_ref, own_ref, r_ref, b_ref, c_ref, p_ref, dq_ref, d0_ref, d1_ref, d2_ref):
    block = q_ref.shape[0]
    column = info_ref[0]
    near = near_block(column, b_ref, c_ref)
    tri_g = triangle(block, GROUP)
    scaling = 1.0 / math.sqrt(HEAD_DIM)
    for g in range(own_ref.shape[1] // HEAD_DIM):
        keys, values = window(g, block, own_ref, r_ref, near)
        queries, grads = stacked(q_ref, g), stacked(do_ref, g)
        w_x = p_ref[g, 0:block].astype(F32)
        w_n = p_ref[g, block : 2 * block]
        w_nf = w_n.astype(F32)
        gw_x = jnp.where(tri_g, dot(values[0], grads, NT), dot(values[2], grads, NT))
        gw_n = dot(values[1], grads, NT)
        delta = jnp.sum(w_x * gw_x + w_nf * gw_n, axis=0, keepdims=True)
        gs_x = w_x * (gw_x - delta) * scaling
        gs_n = (w_nf * (gw_n - delta) * scaling).astype(BF16)
        gs_0 = jnp.where(tri_g, gs_x, 0.0).astype(BF16)
        gs_2 = jnp.where(tri_g, 0.0, gs_x).astype(BF16)
        w_0 = jnp.where(tri_g, w_x, 0.0).astype(BF16)
        w_2 = jnp.where(tri_g, 0.0, w_x).astype(BF16)
        cols = slice(g * HEAD_DIM, (g + 1) * HEAD_DIM)
        d2_ref[0:block, cols] = dot(gs_2, queries, NN).astype(d2_ref.dtype)
        d2_ref[block : 2 * block, cols] = dot(w_2, grads, NN).astype(d2_ref.dtype)
        d1_ref[0:block, cols] = dot(gs_n, queries, NN).astype(d1_ref.dtype)
        d1_ref[block : 2 * block, cols] = dot(w_n, grads, NN).astype(d1_ref.dtype)
        d0_ref[0:block, cols] = dot(gs_0, queries, NN)
        d0_ref[block : 2 * block, cols] = dot(w_0, grads, NN)
        dq = dot(jnp.concatenate([gs_0, gs_n, gs_2], axis=0), jnp.concatenate(keys, axis=0), TN)
        for h in range(GROUP):
            heads = slice((g * GROUP + h) * HEAD_DIM, (g * GROUP + h + 1) * HEAD_DIM)
            dq_ref[:, heads] = dq[h * block : (h + 1) * block].astype(dq_ref.dtype)


def final_kernel(n_ctx, info_ref, d0_ref, b_ref, r_ref, dk_ref, dv_ref):
    block = dk_ref.shape[0]
    column = info_ref[0]
    total = d0_ref[...]
    total = total + jnp.where(lax.rem(column, 2) == 0, b_ref[...].astype(F32), 0.0)
    total = total + jnp.where(column + 2 < n_ctx, r_ref[...].astype(F32), 0.0)
    dk_ref[...] = total[0:block].astype(dk_ref.dtype)
    dv_ref[...] = total[block : 2 * block].astype(dv_ref.dtype)


def join_kernel(n_dp, info_ref, *rest):
    pieces, out_ref, sems = rest[:n_dp], rest[n_dp], rest[n_dp + 1]
    row = info_ref[1]
    copies = []
    for k in range(n_dp):
        source = row ^ k if n_dp & (n_dp - 1) == 0 else lax.rem(row - k + n_dp, n_dp)
        copies.append(pltpu.make_async_copy(pieces[k], out_ref.at[0, 0, source], sems.at[k]))
    for copy in copies:
        copy.start()
    for copy in copies:
        copy.wait()


VMEM = pl.BlockSpec(memory_space=pltpu.VMEM)
SMEM = pl.BlockSpec(memory_space=pltpu.SMEM)
HBM = pl.BlockSpec(memory_space=pl.ANY)


def params():
    return pltpu.CompilerParams(vmem_limit_bytes=32 * 1024 * 1024)


def cost(flops, nbytes):
    return pl.CostEstimate(flops=flops, bytes_accessed=nbytes, transcendentals=0)


def swap(value):
    count = lax.axis_size("ctx")
    return lax.ppermute(value, "ctx", [(i, i ^ 1) for i in range(count)])


def ring(value, steps):
    count = lax.axis_size("ctx")
    return lax.ppermute(value, "ctx", [(i, (i + steps) % count) for i in range(count)])


def exchange(value, k):
    count = lax.axis_size("dp")
    if count & (count - 1) == 0:
        pairs = [(i, i ^ k) for i in range(count)]
    else:
        pairs = [(i, (i + k) % count) for i in range(count)]
    return lax.ppermute(value, "dp", pairs)


def on_device(query_rows, key_rows, value_rows, out_grad, segment_ids, home_rows):
    n_dp, n_ctx = lax.axis_size("dp"), lax.axis_size("ctx")
    query, grad = query_rows[0], out_grad[0]
    block, width = query.shape
    kv_width = key_rows.shape[2]
    heads = kv_width // HEAD_DIM
    home = home_rows[0]
    pieces = home.shape[0]
    capacity = max(2, 2 * pieces // n_dp)
    piece_len = block // pieces
    column = lax.axis_index("ctx")
    info = jnp.stack([column, lax.axis_index("dp")]).astype(jnp.int32)
    seg = jnp.pad(segment_ids.astype(BF16), ((0, SEG_ROWS - 1), (0, kv_width - block)))
    own = jnp.concatenate([key_rows[0], value_rows[0], seg], axis=0)
    far = ring(own, 2)
    beside = swap(own)
    crossed = swap(far)

    pairs = 2 * block * block * GROUP * heads * HEAD_DIM
    outs = pl.pallas_call(
        functools.partial(fwd_kernel, n_dp, capacity),
        out_shape=[jax.ShapeDtypeStruct((heads, 2 * block, GROUP * block), BF16)]
        + [jax.ShapeDtypeStruct((capacity, piece_len, width), BF16)] * n_dp,
        in_specs=[SMEM, SMEM] + [VMEM] * 5,
        out_specs=[VMEM] + [HBM] * n_dp,
        scratch_shapes=[
            pltpu.VMEM((n_dp, capacity, piece_len, width), BF16),
            pltpu.SMEM((n_dp,), jnp.int32),
            pltpu.SemaphoreType.DMA((n_dp,)),
        ],
        compiler_params=params(),
        cost_estimate=cost(6 * pairs, 4 << 20),
        name="attend",
    )(info, home, query, own, far, beside, crossed)
    weights, sends = outs[0], outs[1:]
    arrived = [sends[0]] + [exchange(sends[k], k) for k in range(1, n_dp)]
    dq, d0, d1, d2 = pl.pallas_call(
        bwd_kernel,
        out_shape=[
            jax.ShapeDtypeStruct((block, width), BF16),
            jax.ShapeDtypeStruct((2 * block, kv_width), F32),
            jax.ShapeDtypeStruct((2 * block, kv_width), BF16),
            jax.ShapeDtypeStruct((2 * block, kv_width), BF16),
        ],
        in_specs=[SMEM] + [VMEM] * 7,
        out_specs=[VMEM] * 4,
        compiler_params=params(),
        cost_estimate=cost(12 * pairs, 4 << 20),
        name="gradients",
    )(info, query, grad, own, far, beside, crossed, weights)
    d1_in = swap(d1)
    d2_sum = (d2.astype(F32) + jnp.where(column % 2 == 1, d1_in.astype(F32), 0.0)).astype(BF16)
    d2_in = ring(d2_sum, -2)
    dk, dv = pl.pallas_call(
        functools.partial(final_kernel, n_ctx),
        out_shape=[jax.ShapeDtypeStruct((block, kv_width), BF16)] * 2,
        in_specs=[SMEM] + [VMEM] * 3,
        out_specs=[VMEM] * 2,
        compiler_params=params(),
        cost_estimate=cost(0, 2 << 20),
        name="total",
    )(info, d0, d1_in, d2_in)
    routed = pl.pallas_call(
        functools.partial(join_kernel, n_dp),
        out_shape=jax.ShapeDtypeStruct((1, 1, n_dp, capacity, piece_len, width), BF16),
        in_specs=[SMEM] + [HBM] * n_dp,
        out_specs=HBM,
        scratch_shapes=[pltpu.SemaphoreType.DMA((n_dp,))],
        compiler_params=params(),
        cost_estimate=cost(0, 2 << 20),
        name="join",
    )(info, *arrived)
    return routed, dq[None], dk[None], dv[None]


def solution(mesh):
    rows = P("dp", "ctx", None)
    return jax.shard_map(
        on_device,
        mesh=mesh,
        in_specs=(rows, rows, rows, rows, P("dp", "ctx"), P("dp", "ctx")),
        out_specs=(P("dp", "ctx", None, None, None, None), rows, rows, rows),
        check_vma=False,
    )
```

```python
import functools
import math

import jax
import jax.numpy as jnp
from jax import lax
from jax.experimental import pallas as pl
from jax.experimental.pallas import tpu as pltpu
from jax.sharding import PartitionSpec as P

HEAD_DIM = 128
GROUP = 4
SEG_ROWS = 16
F32 = jnp.float32
BF16 = jnp.bfloat16
NEG = -1e30

NT = (((1,), (1,)), ((), ()))
NN = (((1,), (0,)), ((), ()))
TN = (((0,), (0,)), ((), ()))


def dot(a, b, dims):
    return lax.dot_general(a, b, dims, preferred_element_type=F32)


def stacked(ref, g):
    heads = [
        ref[:, (g * GROUP + h) * HEAD_DIM : (g * GROUP + h + 1) * HEAD_DIM] for h in range(GROUP)
    ]
    return jnp.concatenate(heads, axis=0)


def window(g, block, own_ref, r_ref, near):
    cols = slice(g * HEAD_DIM, (g + 1) * HEAD_DIM)
    keys = (own_ref[0:block, cols], near[0:block, cols], r_ref[0:block, cols])
    values = (
        own_ref[block : 2 * block, cols],
        near[block : 2 * block, cols],
        r_ref[block : 2 * block, cols],
    )
    return keys, values


def near_block(column, b_ref, c_ref):
    return jnp.where(lax.rem(column, 2) == 0, c_ref[...], b_ref[...])


def triangle(block, copies):
    key_pos = lax.broadcasted_iota(jnp.int32, (block, copies * block), 0)
    query_pos = lax.broadcasted_iota(jnp.int32, (block, copies * block), 1)
    return key_pos <= lax.rem(query_pos, block)


def step_between(home, row, count):
    return home ^ row if count & (count - 1) == 0 else lax.rem(home - row + count, count)


def fwd_kernel(n_dp, home_hbm, q_ref, own_ref, r_ref, b_ref, c_ref, *rest):
    p_ref = rest[0]
    sends = rest[1 : 1 + n_dp]
    held, counts, filled, home_ref, sem = rest[1 + n_dp :]
    fetch = pltpu.make_async_copy(home_hbm, home_ref, sem)
    fetch.start()
    block = q_ref.shape[0]
    column, row = lax.axis_index("ctx"), lax.axis_index("dp")
    pieces = home_ref.shape[1]
    piece_len = block // pieces
    capacity = sends[0].shape[0]
    held[pieces] = jnp.zeros(held.shape[1:], held.dtype)
    near = near_block(column, b_ref, c_ref)

    def seg_of(value):
        return value[2 * block : 2 * block + SEG_ROWS, 0:block].astype(F32)[0:1]

    seg_own, seg_near, seg_far = seg_of(own_ref), seg_of(near), seg_of(r_ref)
    first = seg_own[:, 0:1]
    reach = jnp.where(column >= 1, jnp.sum((seg_near == first).astype(F32), axis=1, keepdims=True), 0.0)
    reach = reach + jnp.where(
        column >= 2, jnp.sum((seg_far == first).astype(F32), axis=1, keepdims=True), 0.0
    )
    key_pos = lax.broadcasted_iota(jnp.int32, (block, block), 0).astype(F32)
    tri = triangle(block, 1)
    seg_rows = jnp.broadcast_to(seg_own, (block, block))
    joined = seg_rows == first
    own_ok = seg_rows == seg_rows.T
    far_ok = (key_pos >= 2 * block - reach) & joined
    near_ok = (key_pos >= block - reach) & joined
    bias_x = jnp.where((tri & own_ok) | (~tri & far_ok), 0.0, NEG)
    bias_n = jnp.where(near_ok, 0.0, NEG)
    bias_x = jnp.concatenate([bias_x] * GROUP, axis=1)
    bias_n = jnp.concatenate([bias_n] * GROUP, axis=1)
    tri_g = triangle(block, GROUP)
    scaling = math.log2(math.e) / math.sqrt(HEAD_DIM)

    for g in range(own_ref.shape[1] // HEAD_DIM):
        keys, values = window(g, block, own_ref, r_ref, near)
        queries = stacked(q_ref, g)
        s_x = jnp.where(tri_g, dot(keys[0], queries, NT), dot(keys[2], queries, NT))
        s_x = s_x * scaling + bias_x
        s_n = dot(keys[1], queries, NT) * scaling + bias_n
        highest = jnp.max(jnp.maximum(s_x, s_n), axis=0, keepdims=True)
        e_x = jnp.exp2(s_x - highest)
        e_n = jnp.exp2(s_n - highest)
        inverse = 1.0 / jnp.sum(e_x + e_n, axis=0, keepdims=True)
        w_x = e_x * inverse
        w_n = (e_n * inverse).astype(BF16)
        p_ref[g, 0:block] = w_x.astype(BF16)
        p_ref[g, block : 2 * block] = w_n
        w_0 = jnp.where(tri_g, w_x, 0.0).astype(BF16)
        w_2 = jnp.where(tri_g, 0.0, w_x).astype(BF16)
        weights = jnp.concatenate([w_0, w_n, w_2], axis=0)
        attended = dot(weights, jnp.concatenate(values, axis=0), TN)
        for h in range(GROUP):
            cols = slice((g * GROUP + h) * HEAD_DIM, (g * GROUP + h + 1) * HEAD_DIM)
            tile = attended[h * block : (h + 1) * block].astype(BF16)
            held[0:pieces, :, cols] = tile.reshape(pieces, piece_len, HEAD_DIM)
    fetch.wait()
    for d in range(n_dp):
        counts[d] = 0
        for slot in range(capacity):
            filled[d * capacity + slot] = pieces
    for m in range(pieces):
        step = step_between(home_ref[0, m], row, n_dp)
        slot = counts[step]
        counts[step] = slot + 1
        filled[step * capacity + slot] = m
    for d in range(n_dp):
        for slot in range(capacity):
            sends[d][slot] = held[filled[d * capacity + slot]]


def bwd_kernel(q_ref, do_ref, own_ref, r_ref, b_ref, c_ref, p_ref, dq_ref, d0_ref, d1_ref, d2_ref):
    block = q_ref.shape[0]
    near = near_block(lax.axis_index("ctx"), b_ref, c_ref)
    tri_g = triangle(block, GROUP)
    scaling = 1.0 / math.sqrt(HEAD_DIM)
    for g in range(own_ref.shape[1] // HEAD_DIM):
        keys, values = window(g, block, own_ref, r_ref, near)
        queries, grads = stacked(q_ref, g), stacked(do_ref, g)
        w_x = p_ref[g, 0:block].astype(F32)
        w_n = p_ref[g, block : 2 * block]
        w_nf = w_n.astype(F32)
        gw_x = jnp.where(tri_g, dot(values[0], grads, NT), dot(values[2], grads, NT))
        gw_n = dot(values[1], grads, NT)
        delta = jnp.sum(w_x * gw_x + w_nf * gw_n, axis=0, keepdims=True)
        gs_x = w_x * (gw_x - delta) * scaling
        gs_n = (w_nf * (gw_n - delta) * scaling).astype(BF16)
        gs_0 = jnp.where(tri_g, gs_x, 0.0).astype(BF16)
        gs_2 = jnp.where(tri_g, 0.0, gs_x).astype(BF16)
        w_0 = jnp.where(tri_g, w_x, 0.0).astype(BF16)
        w_2 = jnp.where(tri_g, 0.0, w_x).astype(BF16)
        cols = slice(g * HEAD_DIM, (g + 1) * HEAD_DIM)
        d2_ref[0:block, cols] = dot(gs_2, queries, NN).astype(d2_ref.dtype)
        d2_ref[block : 2 * block, cols] = dot(w_2, grads, NN).astype(d2_ref.dtype)
        d1_ref[0:block, cols] = dot(gs_n, queries, NN).astype(d1_ref.dtype)
        d1_ref[block : 2 * block, cols] = dot(w_n, grads, NN).astype(d1_ref.dtype)
        d0_ref[0:block, cols] = dot(gs_0, queries, NN)
        d0_ref[block : 2 * block, cols] = dot(w_0, grads, NN)
        dq = dot(jnp.concatenate([gs_0, gs_n, gs_2], axis=0), jnp.concatenate(keys, axis=0), TN)
        for h in range(GROUP):
            heads = slice((g * GROUP + h) * HEAD_DIM, (g * GROUP + h + 1) * HEAD_DIM)
            dq_ref[:, heads] = dq[h * block : (h + 1) * block].astype(dq_ref.dtype)


def prep_kernel(seg_hbm, k_hbm, v_hbm, own_ref, seg_ref, sems):
    block = k_hbm.shape[0]
    copies = [
        pltpu.make_async_copy(seg_hbm, seg_ref, sems.at[0]),
        pltpu.make_async_copy(k_hbm, own_ref.at[0:block], sems.at[1]),
        pltpu.make_async_copy(v_hbm, own_ref.at[block : 2 * block], sems.at[2]),
    ]
    for copy in copies:
        copy.start()
    tail = slice(2 * block, 2 * block + SEG_ROWS)
    own_ref[tail, block:] = jnp.zeros((SEG_ROWS, own_ref.shape[1] - block), BF16)
    copies[0].wait()
    ids = jnp.broadcast_to(seg_ref[...].astype(F32), (SEG_ROWS, block))
    own_ref[tail, 0:block] = ids.astype(BF16)
    for copy in copies[1:]:
        copy.wait()


def final_kernel(n_dp, n_ctx, *rest):
    pieces = rest[:n_dp]
    d1_ref, d2_ref, d0_ref, out_ref, dk_ref, dv_ref, total_ref, sems = rest[n_dp:]
    row, column = lax.axis_index("dp"), lax.axis_index("ctx")
    copies = []
    for k in range(n_dp):
        source = row ^ k if n_dp & (n_dp - 1) == 0 else lax.rem(row - k + n_dp, n_dp)
        copies.append(pltpu.make_async_copy(pieces[k], out_ref.at[0, 0, source], sems.at[k]))
    for copy in copies:
        copy.start()
    block = dk_ref.shape[0]
    for part, target in ((0, dk_ref), (1, dv_ref)):
        rows = slice(part * block, (part + 1) * block)
        total = d0_ref[rows]
        total = total + jnp.where(column + 1 < n_ctx, d1_ref[rows].astype(F32), 0.0)
        total = total + jnp.where(column + 2 < n_ctx, d2_ref[rows].astype(F32), 0.0)
        total_ref[rows] = total.astype(total_ref.dtype)
        copies.append(pltpu.make_async_copy(total_ref.at[rows], target, sems.at[n_dp + part]))
        copies[-1].start()
    for copy in copies:
        copy.wait()


VMEM = pl.BlockSpec(memory_space=pltpu.VMEM)
HBM = pl.BlockSpec(memory_space=pl.ANY)


def params(kib=32 * 1024):
    return pltpu.CompilerParams(vmem_limit_bytes=kib * 1024)


def cost(flops, nbytes):
    return pl.CostEstimate(flops=flops, bytes_accessed=nbytes, transcendentals=0)


def pinned(*arrays):
    return [pltpu.with_memory_space_constraint(array, pltpu.HBM) for array in arrays]


def swap(value):
    count = lax.axis_size("ctx")
    return lax.ppermute(value, "ctx", [(i, i ^ 1) for i in range(count)])


def ring(value, steps):
    count = lax.axis_size("ctx")
    return lax.ppermute(value, "ctx", [(i, (i + steps) % count) for i in range(count)])


def exchange(value, k):
    count = lax.axis_size("dp")
    if count & (count - 1) == 0:
        pairs = [(i, i ^ k) for i in range(count)]
    else:
        pairs = [(i, (i + k) % count) for i in range(count)]
    return lax.ppermute(value, "dp", pairs)


def on_device(query_rows, key_rows, value_rows, out_grad, segment_ids, home_rows):
    n_dp, n_ctx = lax.axis_size("dp"), lax.axis_size("ctx")
    query, grad = query_rows[0], out_grad[0]
    block, width = query.shape
    kv_width = key_rows.shape[2]
    heads = kv_width // HEAD_DIM
    pieces = home_rows.shape[1]
    capacity = max(2, 2 * pieces // n_dp)
    piece_len = block // pieces
    column = lax.axis_index("ctx")
    own = pl.pallas_call(
        prep_kernel,
        out_shape=jax.ShapeDtypeStruct((2 * block + SEG_ROWS, kv_width), BF16),
        in_specs=[HBM] * 3,
        out_specs=VMEM,
        scratch_shapes=[pltpu.VMEM((1, block), jnp.int32), pltpu.SemaphoreType.DMA((3,))],
        compiler_params=params(),
        cost_estimate=cost(0, 1 << 19),
        name="bundle",
    )(*pinned(segment_ids, key_rows[0], value_rows[0]))
    far = ring(own, 2)
    beside = swap(own)
    crossed = swap(far)

    pairs = 2 * block * block * GROUP * heads * HEAD_DIM
    outs = pl.pallas_call(
        functools.partial(fwd_kernel, n_dp),
        out_shape=[jax.ShapeDtypeStruct((heads, 2 * block, GROUP * block), BF16)]
        + [jax.ShapeDtypeStruct((capacity, piece_len, width), BF16)] * n_dp,
        in_specs=[HBM] + [VMEM] * 5,
        out_specs=[VMEM] * (1 + n_dp),
        scratch_shapes=[
            pltpu.VMEM((pieces + 1, piece_len, width), BF16),
            pltpu.SMEM((n_dp,), jnp.int32),
            pltpu.SMEM((n_dp * capacity,), jnp.int32),
            pltpu.SMEM((1, pieces), jnp.int32),
            pltpu.SemaphoreType.DMA,
        ],
        compiler_params=params(),
        cost_estimate=cost(6 * pairs, 4 << 20),
        name="attend",
    )(home_rows, query, own, far, beside, crossed)
    weights, sends = outs[0], outs[1:]
    arrived = [sends[0]] + [exchange(sends[k], k) for k in range(1, n_dp)]
    dq, d0, d1, d2 = pl.pallas_call(
        bwd_kernel,
        out_shape=[
            jax.ShapeDtypeStruct((block, width), BF16),
            jax.ShapeDtypeStruct((2 * block, kv_width), F32),
            jax.ShapeDtypeStruct((2 * block, kv_width), BF16),
            jax.ShapeDtypeStruct((2 * block, kv_width), BF16),
        ],
        in_specs=[VMEM] * 7,
        out_specs=[VMEM] * 4,
        compiler_params=params(),
        cost_estimate=cost(12 * pairs, 4 << 20),
        name="gradients",
    )(query, grad, own, far, beside, crossed, weights)
    d1_in, d2_in = ring(d1, -1), ring(d2, -2)
    routed, dk, dv = pl.pallas_call(
        functools.partial(final_kernel, n_dp, n_ctx),
        out_shape=[jax.ShapeDtypeStruct((1, 1, n_dp, capacity, piece_len, width), BF16)]
        + [jax.ShapeDtypeStruct((block, kv_width), BF16)] * 2,
        in_specs=[HBM] * n_dp + [VMEM] * 3,
        out_specs=[HBM] * 3,
        scratch_shapes=[
            pltpu.VMEM((2 * block, kv_width), BF16),
            pltpu.SemaphoreType.DMA((n_dp + 2,)),
        ],
        compiler_params=params(),
        cost_estimate=cost(0, 4 << 20),
        name="finish",
    )(*arrived, d1_in, d2_in, d0)
    return routed, dq[None], dk[None], dv[None]


def solution(mesh):
    rows = P("dp", "ctx", None)
    return jax.shard_map(
        on_device,
        mesh=mesh,
        in_specs=(rows, rows, rows, rows, P("dp", "ctx"), P("dp", "ctx")),
        out_specs=(P("dp", "ctx", None, None, None, None), rows, rows, rows),
        check_vma=False,
    )
```

```python
import functools
import math

import jax
import jax.numpy as jnp
from jax import lax
from jax.experimental import pallas as pl
from jax.experimental.pallas import tpu as pltpu
from jax.sharding import PartitionSpec as P

HEAD_DIM = 128
GROUP = 4
SEG_ROWS = 16
F32 = jnp.float32
BF16 = jnp.bfloat16
NEG = -1e30

NT = (((1,), (1,)), ((), ()))
NN = (((1,), (0,)), ((), ()))
TN = (((0,), (0,)), ((), ()))


def dot(a, b, dims):
    return lax.dot_general(a, b, dims, preferred_element_type=F32)


def stacked(ref, g):
    heads = [
        ref[:, (g * GROUP + h) * HEAD_DIM : (g * GROUP + h + 1) * HEAD_DIM] for h in range(GROUP)
    ]
    return jnp.concatenate(heads, axis=0)


def window(g, block, own_ref, far, near):
    cols = slice(g * HEAD_DIM, (g + 1) * HEAD_DIM)
    keys = (own_ref[0:block, cols], near[0:block, cols], far[0:block, cols])
    values = (
        own_ref[block : 2 * block, cols],
        near[block : 2 * block, cols],
        far[block : 2 * block, cols],
    )
    return keys, values


def near_block(column, b_ref, c_ref):
    return jnp.where(lax.rem(column, 2) == 0, c_ref[...], b_ref[...])


def triangle(block, copies):
    key_pos = lax.broadcasted_iota(jnp.int32, (block, copies * block), 0)
    query_pos = lax.broadcasted_iota(jnp.int32, (block, copies * block), 1)
    return key_pos <= lax.rem(query_pos, block)


def step_between(home, row, count):
    return home ^ row if count & (count - 1) == 0 else lax.rem(home - row + count, count)


def fwd_kernel(n_dp, home_hbm, q_ref, own_ref, r_ref, b_ref, c_ref, *rest):
    p_ref = rest[0]
    sends = rest[1 : 1 + n_dp]
    held, counts, filled, home_ref, sem = rest[1 + n_dp :]
    fetch = pltpu.make_async_copy(home_hbm, home_ref, sem)
    fetch.start()
    block = q_ref.shape[0]
    column, row = lax.axis_index("ctx"), lax.axis_index("dp")
    pieces = home_ref.shape[1]
    piece_len = block // pieces
    capacity = sends[0].shape[0]
    held[pieces] = jnp.zeros(held.shape[1:], held.dtype)
    near = near_block(column, b_ref, c_ref)

    def seg_of(value):
        return value[2 * block : 2 * block + SEG_ROWS, 0:block].astype(F32)[0:1]

    seg_own, seg_near, seg_far = seg_of(own_ref), seg_of(near), seg_of(r_ref)
    first = seg_own[:, 0:1]
    reach = jnp.where(column >= 1, jnp.sum((seg_near == first).astype(F32), axis=1, keepdims=True), 0.0)
    reach = reach + jnp.where(
        column >= 2, jnp.sum((seg_far == first).astype(F32), axis=1, keepdims=True), 0.0
    )
    key_pos = lax.broadcasted_iota(jnp.int32, (block, block), 0).astype(F32)
    tri = triangle(block, 1)
    seg_rows = jnp.broadcast_to(seg_own, (block, block))
    joined = seg_rows == first
    own_ok = seg_rows == seg_rows.T
    far_ok = (key_pos >= 2 * block - reach) & joined
    near_ok = (key_pos >= block - reach) & joined
    bias_x = jnp.where((tri & own_ok) | (~tri & far_ok), 0.0, NEG)
    bias_n = jnp.where(near_ok, 0.0, NEG)
    bias_x = jnp.concatenate([bias_x] * GROUP, axis=1)
    bias_n = jnp.concatenate([bias_n] * GROUP, axis=1)
    tri_g = triangle(block, GROUP)
    scaling = math.log2(math.e) / math.sqrt(HEAD_DIM)

    for g in range(own_ref.shape[1] // HEAD_DIM):
        keys, values = window(g, block, own_ref, r_ref, near)
        queries = stacked(q_ref, g)
        s_x = jnp.where(tri_g, dot(keys[0], queries, NT), dot(keys[2], queries, NT))
        s_x = s_x * scaling + bias_x
        s_n = dot(keys[1], queries, NT) * scaling + bias_n
        highest = jnp.max(jnp.maximum(s_x, s_n), axis=0, keepdims=True)
        e_x = jnp.exp2(s_x - highest)
        e_n = jnp.exp2(s_n - highest)
        inverse = 1.0 / jnp.sum(e_x + e_n, axis=0, keepdims=True)
        w_x = e_x * inverse
        w_n = (e_n * inverse).astype(BF16)
        p_ref[g, 0:block] = w_x.astype(BF16)
        p_ref[g, block : 2 * block] = w_n
        w_0 = jnp.where(tri_g, w_x, 0.0).astype(BF16)
        w_2 = jnp.where(tri_g, 0.0, w_x).astype(BF16)
        weights = jnp.concatenate([w_0, w_n, w_2], axis=0)
        attended = dot(weights, jnp.concatenate(values, axis=0), TN)
        for h in range(GROUP):
            cols = slice((g * GROUP + h) * HEAD_DIM, (g * GROUP + h + 1) * HEAD_DIM)
            tile = attended[h * block : (h + 1) * block].astype(BF16)
            held[0:pieces, :, cols] = tile.reshape(pieces, piece_len, HEAD_DIM)
    fetch.wait()
    for d in range(n_dp):
        counts[d] = 0
        for slot in range(capacity):
            filled[d * capacity + slot] = pieces
    for m in range(pieces):
        step = step_between(home_ref[0, m], row, n_dp)
        slot = counts[step]
        counts[step] = slot + 1
        filled[step * capacity + slot] = m
    for d in range(n_dp):
        for slot in range(capacity):
            sends[d][slot] = held[filled[d * capacity + slot]]


def split(tri, packed):
    own = jnp.where(tri, packed, 0.0).astype(BF16)
    far = jnp.where(tri, 0.0, packed).astype(BF16)
    return own, far


def sent_kernel(q_ref, do_ref, own_ref, r_ref, b_ref, c_ref, p_ref, gs_ref, d2_ref, dk1_ref, dv1_ref):
    block = q_ref.shape[0]
    near = near_block(lax.axis_index("ctx"), b_ref, c_ref)
    tri_g = triangle(block, GROUP)
    scaling = 1.0 / math.sqrt(HEAD_DIM)
    for g in range(own_ref.shape[1] // HEAD_DIM):
        _, values = window(g, block, own_ref, r_ref, near)
        queries, grads = stacked(q_ref, g), stacked(do_ref, g)
        w_x = p_ref[g, 0:block].astype(F32)
        w_n = p_ref[g, block : 2 * block]
        w_nf = w_n.astype(F32)
        gw_x = jnp.where(tri_g, dot(values[0], grads, NT), dot(values[2], grads, NT))
        gw_n = dot(values[1], grads, NT)
        delta = jnp.sum(w_x * gw_x + w_nf * gw_n, axis=0, keepdims=True)
        gs_x = w_x * (gw_x - delta) * scaling
        gs_n = (w_nf * (gw_n - delta) * scaling).astype(BF16)
        gs_ref[g, 0:block] = gs_x.astype(BF16)
        gs_ref[g, block : 2 * block] = gs_n
        _, gs_2 = split(tri_g, gs_x)
        _, w_2 = split(tri_g, w_x)
        cols = slice(g * HEAD_DIM, (g + 1) * HEAD_DIM)
        dk1_ref[:, cols] = dot(gs_n, queries, NN).astype(dk1_ref.dtype)
        dv1_ref[:, cols] = dot(w_n, grads, NN).astype(dv1_ref.dtype)
        d2_ref[0:block, cols] = dot(gs_2, queries, NN).astype(d2_ref.dtype)
        d2_ref[block : 2 * block, cols] = dot(w_2, grads, NN).astype(d2_ref.dtype)


def kept_kernel(q_ref, do_ref, own_ref, r_ref, b_ref, c_ref, p_ref, gs_ref, dq_ref, d0_ref, mark_ref):
    mark_ref[...] = jnp.zeros_like(mark_ref)
    block = q_ref.shape[0]
    near = near_block(lax.axis_index("ctx"), b_ref, c_ref)
    tri_g = triangle(block, GROUP)
    for g in range(own_ref.shape[1] // HEAD_DIM):
        keys, _ = window(g, block, own_ref, r_ref, near)
        queries, grads = stacked(q_ref, g), stacked(do_ref, g)
        gs_0, gs_2 = split(tri_g, gs_ref[g, 0:block].astype(F32))
        w_0, _ = split(tri_g, p_ref[g, 0:block].astype(F32))
        gs_n = gs_ref[g, block : 2 * block]
        cols = slice(g * HEAD_DIM, (g + 1) * HEAD_DIM)
        d0_ref[0:block, cols] = dot(gs_0, queries, NN)
        d0_ref[block : 2 * block, cols] = dot(w_0, grads, NN)
        dq = dot(jnp.concatenate([gs_0, gs_n, gs_2], axis=0), jnp.concatenate(keys, axis=0), TN)
        for h in range(GROUP):
            heads = slice((g * GROUP + h) * HEAD_DIM, (g * GROUP + h + 1) * HEAD_DIM)
            dq_ref[:, heads] = dq[h * block : (h + 1) * block].astype(dq_ref.dtype)


def prep_kernel(seg_hbm, k_hbm, v_hbm, own_ref, seg_ref, sems):
    block = k_hbm.shape[0]
    copies = [
        pltpu.make_async_copy(seg_hbm, seg_ref, sems.at[0]),
        pltpu.make_async_copy(k_hbm, own_ref.at[0:block], sems.at[1]),
        pltpu.make_async_copy(v_hbm, own_ref.at[block : 2 * block], sems.at[2]),
    ]
    for copy in copies:
        copy.start()
    tail = slice(2 * block, 2 * block + SEG_ROWS)
    own_ref[tail, block:] = jnp.zeros((SEG_ROWS, own_ref.shape[1] - block), BF16)
    copies[0].wait()
    ids = jnp.broadcast_to(seg_ref[...].astype(F32), (SEG_ROWS, block))
    own_ref[tail, 0:block] = ids.astype(BF16)
    for copy in copies[1:]:
        copy.wait()


def merge_kernel(d2_ref, dk1_ref, dv1_ref, out_ref):
    block = dk1_ref.shape[0]
    odd = lax.rem(lax.axis_index("ctx"), 2) == 1
    for part, d1_ref in enumerate((dk1_ref, dv1_ref)):
        rows = slice(part * block, (part + 1) * block)
        other = jnp.where(odd, d1_ref[...].astype(F32), 0.0)
        out_ref[rows] = (d2_ref[rows].astype(F32) + other).astype(out_ref.dtype)


def join_kernel(n_dp, *rest):
    pieces, (_, out_ref, mark_ref, sems) = rest[:n_dp], rest[n_dp:]
    row = lax.axis_index("dp")
    copies = []
    for k in range(n_dp):
        source = row ^ k if n_dp & (n_dp - 1) == 0 else lax.rem(row - k + n_dp, n_dp)
        copies.append(pltpu.make_async_copy(pieces[n_dp - 1 - k], out_ref.at[0, 0, source], sems.at[k]))
    for copy in copies:
        copy.start()
    mark_ref[...] = jnp.zeros_like(mark_ref)
    for copy in copies:
        copy.wait()


def total_kernel(n_ctx, d0_ref, dk1_ref, dv1_ref, uneven_ref, even_ref, _, dk_ref, dv_ref, total_ref, sems):
    column = lax.axis_index("ctx")
    block = dk_ref.shape[0]
    copies = []
    for part, (d1_ref, target) in enumerate(((dk1_ref, dk_ref), (dv1_ref, dv_ref))):
        rows = slice(part * block, (part + 1) * block)
        total = d0_ref[rows]
        total = total + jnp.where(lax.rem(column, 2) == 0, d1_ref[...].astype(F32), 0.0)
        d2 = jnp.where(lax.rem(column // 2, 2) == 0, even_ref[rows], uneven_ref[rows])
        total = total + jnp.where(column + 2 < n_ctx, d2.astype(F32), 0.0)
        total_ref[rows] = total.astype(total_ref.dtype)
        copies.append(pltpu.make_async_copy(total_ref.at[rows], target, sems.at[part]))
        copies[-1].start()
    for copy in copies:
        copy.wait()


VMEM = pl.BlockSpec(memory_space=pltpu.VMEM)
HBM = pl.BlockSpec(memory_space=pl.ANY)


def params(kib=32 * 1024):
    return pltpu.CompilerParams(vmem_limit_bytes=kib * 1024)


def cost(flops, nbytes):
    return pl.CostEstimate(flops=flops, bytes_accessed=nbytes, transcendentals=0)


def pinned(*arrays):
    return [pltpu.with_memory_space_constraint(array, pltpu.HBM) for array in arrays]


def swap(value):
    count = lax.axis_size("ctx")
    return lax.ppermute(value, "ctx", [(i, i ^ 1) for i in range(count)])


def from_chip(value):
    count = lax.axis_size("ctx")

    def pairs(first):
        found = []
        for i in range(count):
            chip = i // 2
            other = chip + 1 if (chip - first) % 2 == 0 else chip - 1
            found.append((i, 2 * other + i % 2 if 0 <= other < count // 2 else i ^ 1))
        return found

    return lax.ppermute(value, "ctx", pairs(0)), lax.ppermute(value, "ctx", pairs(1))


def exchange(value, k):
    count = lax.axis_size("dp")
    if count & (count - 1) == 0:
        pairs = [(i, i ^ k) for i in range(count)]
    else:
        pairs = [(i, (i + k) % count) for i in range(count)]
    return lax.ppermute(value, "dp", pairs)


def on_device(query_rows, key_rows, value_rows, out_grad, segment_ids, home_rows):
    n_dp, n_ctx = lax.axis_size("dp"), lax.axis_size("ctx")
    query, grad = query_rows[0], out_grad[0]
    block, width = query.shape
    kv_width = key_rows.shape[2]
    heads = kv_width // HEAD_DIM
    pieces = home_rows.shape[1]
    capacity = max(2, 2 * pieces // n_dp)
    piece_len = block // pieces
    column = lax.axis_index("ctx")
    own = pl.pallas_call(
        prep_kernel,
        out_shape=jax.ShapeDtypeStruct((2 * block + SEG_ROWS, kv_width), BF16),
        in_specs=[HBM] * 3,
        out_specs=VMEM,
        scratch_shapes=[pltpu.VMEM((1, block), jnp.int32), pltpu.SemaphoreType.DMA((3,))],
        compiler_params=params(),
        cost_estimate=cost(0, 1 << 19),
        name="bundle",
    )(*pinned(segment_ids, key_rows[0], value_rows[0]))
    even, uneven = from_chip(own)
    far = jnp.where(lax.rem(column // 2, 2) == 0, uneven, even)
    beside = swap(own)
    crossed = swap(far)

    pairs = 2 * block * block * GROUP * heads * HEAD_DIM
    outs = pl.pallas_call(
        functools.partial(fwd_kernel, n_dp),
        out_shape=[jax.ShapeDtypeStruct((heads, 2 * block, GROUP * block), BF16)]
        + [jax.ShapeDtypeStruct((capacity, piece_len, width), BF16)] * n_dp,
        in_specs=[HBM] + [VMEM] * 5,
        out_specs=[VMEM] * (1 + n_dp),
        scratch_shapes=[
            pltpu.VMEM((pieces + 1, piece_len, width), BF16),
            pltpu.SMEM((n_dp,), jnp.int32),
            pltpu.SMEM((n_dp * capacity,), jnp.int32),
            pltpu.SMEM((1, pieces), jnp.int32),
            pltpu.SemaphoreType.DMA,
        ],
        compiler_params=params(),
        cost_estimate=cost(6 * pairs, 4 << 20),
        name="attend",
    )(home_rows, query, own, far, beside, crossed)
    weights, sends = outs[0], outs[1:]
    arrived = [exchange(sends[k], k) for k in range(n_dp - 1, 0, -1)] + [sends[0]]
    terms = jax.ShapeDtypeStruct((2 * block, kv_width), BF16)
    half = jax.ShapeDtypeStruct((block, kv_width), BF16)
    mark = jax.ShapeDtypeStruct((8, HEAD_DIM), F32)
    score_grads, d2, dk1, dv1 = pl.pallas_call(
        sent_kernel,
        out_shape=[jax.ShapeDtypeStruct(weights.shape, BF16), terms, half, half],
        in_specs=[VMEM] * 7,
        out_specs=[VMEM] * 4,
        compiler_params=params(),
        cost_estimate=cost(7 * pairs, 4 << 20),
        name="sent_terms",
    )(query, grad, own, far, beside, crossed, weights)
    dq, d0, after_kept = pl.pallas_call(
        kept_kernel,
        out_shape=[
            jax.ShapeDtypeStruct((block, width), BF16),
            jax.ShapeDtypeStruct((2 * block, kv_width), F32),
            mark,
        ],
        in_specs=[VMEM] * 8,
        out_specs=[VMEM] * 3,
        compiler_params=params(),
        cost_estimate=cost(1073741824, 0),
        name="kept_terms",
    )(query, grad, own, far, beside, crossed, weights, score_grads)
    dk1_in, dv1_in = swap(dk1), swap(dv1)
    d2_sum = pl.pallas_call(
        merge_kernel,
        out_shape=terms,
        in_specs=[VMEM] * 3,
        out_specs=VMEM,
        compiler_params=params(),
        cost_estimate=cost(0, 0),
        name="merge",
    )(d2, dk1_in, dv1_in)
    d2_even, d2_uneven = from_chip(d2_sum)
    routed, after_join = pl.pallas_call(
        functools.partial(join_kernel, n_dp),
        out_shape=[jax.ShapeDtypeStruct((1, 1, n_dp, capacity, piece_len, width), BF16), mark],
        in_specs=[HBM] * (n_dp + 1),
        out_specs=[HBM, VMEM],
        scratch_shapes=[pltpu.SemaphoreType.DMA((n_dp,))],
        compiler_params=params(),
        cost_estimate=cost(2147483648, 0),
        name="join",
    )(*arrived, after_kept)
    dk, dv = pl.pallas_call(
        functools.partial(total_kernel, n_ctx),
        out_shape=[jax.ShapeDtypeStruct((block, kv_width), BF16)] * 2,
        in_specs=[VMEM] * 5 + [HBM],
        out_specs=[HBM] * 2,
        scratch_shapes=[
            pltpu.VMEM((2 * block, kv_width), BF16),
            pltpu.SemaphoreType.DMA((2,)),
        ],
        compiler_params=params(),
        cost_estimate=cost(0, 1 << 20),
        name="total",
    )(d0, dk1_in, dv1_in, d2_uneven, d2_even, after_join)
    return routed, dq[None], dk[None], dv[None]


def solution(mesh):
    rows = P("dp", "ctx", None)
    return jax.shard_map(
        on_device,
        mesh=mesh,
        in_specs=(rows, rows, rows, rows, P("dp", "ctx"), P("dp", "ctx")),
        out_specs=(P("dp", "ctx", None, None, None, None), rows, rows, rows),
        check_vma=False,
    )
```

```python
import functools
import math

import jax
import jax.numpy as jnp
from jax import lax
from jax.experimental import pallas as pl
from jax.experimental.pallas import tpu as pltpu
from jax.sharding import PartitionSpec as P

HEAD_DIM = 128
GROUP = 4
SEG_ROWS = 16
F32 = jnp.float32
BF16 = jnp.bfloat16
NEG = -1e30

NT = (((1,), (1,)), ((), ()))
NN = (((1,), (0,)), ((), ()))
TN = (((0,), (0,)), ((), ()))


def dot(a, b, dims):
    return lax.dot_general(a, b, dims, preferred_element_type=F32)


def stacked(ref, g):
    heads = [
        ref[:, (g * GROUP + h) * HEAD_DIM : (g * GROUP + h + 1) * HEAD_DIM] for h in range(GROUP)
    ]
    return jnp.concatenate(heads, axis=0)


def window(g, block, own_ref, far_ref, near_ref):
    cols = slice(g * HEAD_DIM, (g + 1) * HEAD_DIM)
    keys = (own_ref[0:block, cols], near_ref[0:block, cols], far_ref[0:block, cols])
    values = (
        own_ref[block : 2 * block, cols],
        near_ref[block : 2 * block, cols],
        far_ref[block : 2 * block, cols],
    )
    return keys, values


def triangle(block, copies):
    key_pos = lax.broadcasted_iota(jnp.int32, (block, copies * block), 0)
    query_pos = lax.broadcasted_iota(jnp.int32, (block, copies * block), 1)
    return key_pos <= lax.rem(query_pos, block)


def step_between(home, row, count):
    return home ^ row if count & (count - 1) == 0 else lax.rem(home - row + count, count)


def fwd_kernel(n_dp, home_hbm, qt_ref, s0_ref, own_ref, far_ref, near_ref, *rest):
    p_ref = rest[0]
    sends = rest[1 : 1 + n_dp]
    held, counts, filled, home_ref, sem = rest[1 + n_dp :]
    fetch = pltpu.make_async_copy(home_hbm, home_ref, sem)
    fetch.start()
    block = s0_ref.shape[1]
    column, row = lax.axis_index("ctx"), lax.axis_index("dp")
    pieces = home_ref.shape[1]
    piece_len = block // pieces
    capacity = sends[0].shape[0]
    held[pieces] = jnp.zeros(held.shape[1:], held.dtype)

    def seg_of(value):
        return value[2 * block : 2 * block + SEG_ROWS, 0:block].astype(F32)[0:1]

    seg_own, seg_near, seg_far = seg_of(own_ref), seg_of(near_ref), seg_of(far_ref)
    first = seg_own[:, 0:1]
    reach = jnp.where(column >= 1, jnp.sum((seg_near == first).astype(F32), axis=1, keepdims=True), 0.0)
    reach = reach + jnp.where(
        column >= 2, jnp.sum((seg_far == first).astype(F32), axis=1, keepdims=True), 0.0
    )
    key_pos = lax.broadcasted_iota(jnp.int32, (block, block), 0).astype(F32)
    tri = triangle(block, 1)
    seg_rows = jnp.broadcast_to(seg_own, (block, block))
    joined = seg_rows == first
    own_ok = seg_rows == seg_rows.T
    far_ok = (key_pos >= 2 * block - reach) & joined
    near_ok = (key_pos >= block - reach) & joined
    bias_x = jnp.where((tri & own_ok) | (~tri & far_ok), 0.0, NEG)
    bias_n = jnp.where(near_ok, 0.0, NEG)
    bias_x = jnp.concatenate([bias_x] * GROUP, axis=1)
    bias_n = jnp.concatenate([bias_n] * GROUP, axis=1)
    tri_g, lower = triangle(block, GROUP), lower_mask(block)
    scaling = math.log2(math.e) / math.sqrt(HEAD_DIM)

    for g in range(own_ref.shape[1] // HEAD_DIM):
        keys, values = window(g, block, own_ref, far_ref, near_ref)
        scores = dot(jnp.concatenate(keys[1:], axis=0), qt_ref[g], NN)
        s_x = jnp.where(tri_g, s0_ref[g], scores[block:]) * scaling + bias_x
        s_n = scores[0:block] * scaling + bias_n
        highest = jnp.max(jnp.maximum(s_x, s_n), axis=0, keepdims=True)
        e_x = jnp.exp2(s_x - highest)
        e_n = jnp.exp2(s_n - highest)
        inverse = 1.0 / jnp.sum(e_x + e_n, axis=0, keepdims=True)
        w_x = (e_x * inverse).astype(BF16)
        w_n = (e_n * inverse).astype(BF16)
        p_ref[g, 0:block] = w_x
        p_ref[g, block : 2 * block] = w_n
        w_0, w_2 = split(lower, w_x)
        weights = jnp.concatenate([w_0, w_n, w_2], axis=0)
        attended = dot(jnp.concatenate(values, axis=0), weights, TN).astype(BF16)
        for h in range(GROUP):
            cols = slice((g * GROUP + h) * HEAD_DIM, (g * GROUP + h + 1) * HEAD_DIM)
            tile = attended[:, h * block : (h + 1) * block].T
            held[0:pieces, :, cols] = tile.reshape(pieces, piece_len, HEAD_DIM)
    fetch.wait()
    for d in range(n_dp):
        counts[d] = 0
        for slot in range(capacity):
            filled[d * capacity + slot] = pieces
    for m in range(pieces):
        step = step_between(home_ref[0, m], row, n_dp)
        slot = counts[step]
        counts[step] = slot + 1
        filled[step * capacity + slot] = m
    for d in range(n_dp):
        for slot in range(capacity):
            sends[d][slot] = held[filled[d * capacity + slot]]


def split(lower, packed):
    own = packed * lower
    return own, packed - own


def lower_mask(block):
    return jnp.where(triangle(block, GROUP), 1.0, 0.0).astype(BF16)


def ahead_kernel(home_ref, q_ref, do_ref, own_ref, plan_ref, qt_ref, gt_ref, s0_ref, gw0_ref):
    plan_ref[...] = home_ref[...]
    block = q_ref.shape[0]
    for g in range(own_ref.shape[1] // HEAD_DIM):
        cols = slice(g * HEAD_DIM, (g + 1) * HEAD_DIM)
        for source, turned, product, rows in (
            (q_ref, qt_ref, s0_ref, slice(0, block)),
            (do_ref, gt_ref, gw0_ref, slice(block, 2 * block)),
        ):
            turned[g] = stacked(source, g).T
            product[g] = dot(own_ref[rows, cols], turned[g], NN)


def sent_kernel(q_ref, do_ref, gt_ref, gw0_ref, own_ref, far_ref, near_ref, p_ref, gs_ref, d2_ref, dk1_ref, dv1_ref):
    block = q_ref.shape[0]
    tri_g, lower = triangle(block, GROUP), lower_mask(block)
    scaling = 1.0 / math.sqrt(HEAD_DIM)
    for g in range(own_ref.shape[1] // HEAD_DIM):
        _, values = window(g, block, own_ref, far_ref, near_ref)
        queries, grads = stacked(q_ref, g), stacked(do_ref, g)
        w_xb = p_ref[g, 0:block]
        w_x = w_xb.astype(F32)
        w_n = p_ref[g, block : 2 * block]
        w_nf = w_n.astype(F32)
        score_terms = dot(jnp.concatenate(values[1:], axis=0), gt_ref[g], NN)
        gw_x = jnp.where(tri_g, gw0_ref[g], score_terms[block:])
        gw_n = score_terms[0:block]
        delta = jnp.sum(w_x * gw_x + w_nf * gw_n, axis=0, keepdims=True)
        gs_x = (w_x * (gw_x - delta) * scaling).astype(BF16)
        gs_n = (w_nf * (gw_n - delta) * scaling).astype(BF16)
        gs_ref[g, 0:block] = gs_x
        gs_ref[g, block : 2 * block] = gs_n
        _, gs_2 = split(lower, gs_x)
        _, w_2 = split(lower, w_xb)
        cols = slice(g * HEAD_DIM, (g + 1) * HEAD_DIM)
        dk = dot(jnp.concatenate([gs_n, gs_2], axis=0), queries, NN).astype(d2_ref.dtype)
        dv = dot(jnp.concatenate([w_n, w_2], axis=0), grads, NN).astype(d2_ref.dtype)
        dk1_ref[:, cols] = dk[0:block]
        dv1_ref[:, cols] = dv[0:block]
        d2_ref[0:block, cols] = dk[block:]
        d2_ref[block : 2 * block, cols] = dv[block:]


def kept_kernel(q_ref, do_ref, own_ref, far_ref, near_ref, p_ref, gs_ref, dq_ref, d0_ref, mark_ref):
    mark_ref[...] = jnp.zeros_like(mark_ref)
    block = q_ref.shape[0]
    lower = lower_mask(block)
    for g in range(own_ref.shape[1] // HEAD_DIM):
        keys, _ = window(g, block, own_ref, far_ref, near_ref)
        queries, grads = stacked(q_ref, g), stacked(do_ref, g)
        gs_0, gs_2 = split(lower, gs_ref[g, 0:block])
        w_0, _ = split(lower, p_ref[g, 0:block])
        gs_n = gs_ref[g, block : 2 * block]
        cols = slice(g * HEAD_DIM, (g + 1) * HEAD_DIM)
        d0_ref[0:block, cols] = dot(gs_0, queries, NN)
        d0_ref[block : 2 * block, cols] = dot(w_0, grads, NN)
        dq = dot(jnp.concatenate([gs_0, gs_n, gs_2], axis=0), jnp.concatenate(keys, axis=0), TN)
        for h in range(GROUP):
            heads = slice((g * GROUP + h) * HEAD_DIM, (g * GROUP + h + 1) * HEAD_DIM)
            dq_ref[:, heads] = dq[h * block : (h + 1) * block].astype(dq_ref.dtype)


def prep_kernel(seg_hbm, k_hbm, v_hbm, own_ref, seg_ref, sems):
    block = k_hbm.shape[0]
    copies = [
        pltpu.make_async_copy(seg_hbm, seg_ref, sems.at[0]),
        pltpu.make_async_copy(k_hbm, own_ref.at[0:block], sems.at[1]),
        pltpu.make_async_copy(v_hbm, own_ref.at[block : 2 * block], sems.at[2]),
    ]
    for copy in copies:
        copy.start()
    tail = slice(2 * block, 2 * block + SEG_ROWS)
    own_ref[tail, block:] = jnp.zeros((SEG_ROWS, own_ref.shape[1] - block), BF16)
    copies[0].wait()
    ids = jnp.broadcast_to(seg_ref[...].astype(F32), (SEG_ROWS, block))
    own_ref[tail, 0:block] = ids.astype(BF16)
    for copy in copies[1:]:
        copy.wait()


def merge_kernel(d2_ref, dk1_ref, dv1_ref, out_ref):
    block = dk1_ref.shape[0]
    odd = lax.rem(lax.axis_index("ctx"), 2) == 1
    for part, d1_ref in enumerate((dk1_ref, dv1_ref)):
        rows = slice(part * block, (part + 1) * block)
        other = jnp.where(odd, d1_ref[...].astype(F32), 0.0)
        out_ref[rows] = (d2_ref[rows].astype(F32) + other).astype(out_ref.dtype)


def source_row(row, step, count):
    return row ^ step if count & (count - 1) == 0 else lax.rem(row - step + count, count)


def early_kernel(n_dp, kept_ref, far_ref, own_ref, out_ref, sems):
    row = lax.axis_index("dp")
    copies = [
        pltpu.make_async_copy(own_ref, out_ref.at[0, 0, row], sems.at[0]),
        pltpu.make_async_copy(
            far_ref, out_ref.at[0, 0, source_row(row, n_dp - 1, n_dp)], sems.at[1]
        ),
    ]
    for copy in copies:
        copy.start()
    for copy in copies:
        copy.wait()


def finish_kernel(n_dp, n_ctx, *rest):
    pieces, rest = rest[: n_dp - 2], rest[n_dp - 2 :]
    uneven_ref, even_ref, dk1_ref, dv1_ref, d0_ref, _, out_ref, dk_ref, dv_ref, total_ref, sems = rest
    row, column = lax.axis_index("dp"), lax.axis_index("ctx")
    block = dk_ref.shape[0]
    copies = []
    for i in range(n_dp - 2):
        target = out_ref.at[0, 0, source_row(row, n_dp - 2 - i, n_dp)]
        copies.append(pltpu.make_async_copy(pieces[i], target, sems.at[i]))
        copies[-1].start()
    for part, (d1_ref, target) in enumerate(((dk1_ref, dk_ref), (dv1_ref, dv_ref))):
        rows = slice(part * block, (part + 1) * block)
        total = d0_ref[rows]
        total = total + jnp.where(lax.rem(column, 2) == 0, d1_ref[...].astype(F32), 0.0)
        d2 = jnp.where(lax.rem(column // 2, 2) == 0, even_ref[rows], uneven_ref[rows])
        total = total + jnp.where(column + 2 < n_ctx, d2.astype(F32), 0.0)
        total_ref[rows] = total.astype(total_ref.dtype)
        copies.append(pltpu.make_async_copy(total_ref.at[rows], target, sems.at[n_dp - 2 + part]))
        copies[-1].start()
    for copy in copies:
        copy.wait()


VMEM = pl.BlockSpec(memory_space=pltpu.VMEM)
HBM = pl.BlockSpec(memory_space=pl.ANY)


def params(kib=32 * 1024):
    return pltpu.CompilerParams(vmem_limit_bytes=kib * 1024)


def cost(flops, nbytes):
    return pl.CostEstimate(flops=flops, bytes_accessed=nbytes, transcendentals=0)


def pinned(*arrays):
    return [pltpu.with_memory_space_constraint(array, pltpu.HBM) for array in arrays]


def swap(value):
    count = lax.axis_size("ctx")
    return lax.ppermute(value, "ctx", [(i, i ^ 1) for i in range(count)])


def from_chip(value):
    count = lax.axis_size("ctx")

    def pairs(first):
        found = []
        for i in range(count):
            chip = i // 2
            other = chip + 1 if (chip - first) % 2 == 0 else chip - 1
            found.append((i, 2 * other + i % 2 if 0 <= other < count // 2 else i ^ 1))
        return found

    return lax.ppermute(value, "ctx", pairs(0)), lax.ppermute(value, "ctx", pairs(1))


def exchange(value, k):
    count = lax.axis_size("dp")
    if count & (count - 1) == 0:
        pairs = [(i, i ^ k) for i in range(count)]
    else:
        pairs = [(i, (i + k) % count) for i in range(count)]
    return lax.ppermute(value, "dp", pairs)


def on_device(query_rows, key_rows, value_rows, out_grad, segment_ids, home_rows):
    n_dp, n_ctx = lax.axis_size("dp"), lax.axis_size("ctx")
    query, grad = query_rows[0], out_grad[0]
    block, width = query.shape
    kv_width = key_rows.shape[2]
    heads = kv_width // HEAD_DIM
    pieces = home_rows.shape[1]
    capacity = max(2, 2 * pieces // n_dp)
    piece_len = block // pieces
    column = lax.axis_index("ctx")
    own = pl.pallas_call(
        prep_kernel,
        out_shape=jax.ShapeDtypeStruct((2 * block + SEG_ROWS, kv_width), BF16),
        in_specs=[HBM] * 3,
        out_specs=VMEM,
        scratch_shapes=[pltpu.VMEM((1, block), jnp.int32), pltpu.SemaphoreType.DMA((3,))],
        compiler_params=params(),
        cost_estimate=cost(0, 1 << 19),
        name="bundle",
    )(*pinned(segment_ids, key_rows[0], value_rows[0]))
    even, uneven = from_chip(own)
    far = jnp.where(lax.rem(column // 2, 2) == 0, uneven, even)
    beside = swap(own)
    near = jnp.where(lax.rem(column, 2) == 0, swap(far), beside)

    pairs = 2 * block * block * GROUP * heads * HEAD_DIM
    turned = jax.ShapeDtypeStruct((heads, HEAD_DIM, GROUP * block), BF16)
    product = jax.ShapeDtypeStruct((heads, block, GROUP * block), F32)
    plan, turned_query, turned_grad, own_scores, own_terms = pl.pallas_call(
        ahead_kernel,
        out_shape=[
            jax.ShapeDtypeStruct(home_rows.shape, jnp.int32), turned, turned, product, product
        ],
        in_specs=[VMEM] * 4,
        out_specs=[VMEM] * 5,
        compiler_params=params(),
        cost_estimate=cost(2 * pairs, 4 << 20),
        name="ahead",
    )(home_rows, query, grad, own)
    outs = pl.pallas_call(
        functools.partial(fwd_kernel, n_dp),
        out_shape=[jax.ShapeDtypeStruct((heads, 2 * block, GROUP * block), BF16)]
        + [jax.ShapeDtypeStruct((capacity, piece_len, width), BF16)] * n_dp,
        in_specs=[HBM] + [VMEM] * 5,
        out_specs=[VMEM] * (1 + n_dp),
        scratch_shapes=[
            pltpu.VMEM((pieces + 1, piece_len, width), BF16),
            pltpu.SMEM((n_dp,), jnp.int32),
            pltpu.SMEM((n_dp * capacity,), jnp.int32),
            pltpu.SMEM((1, pieces), jnp.int32),
            pltpu.SemaphoreType.DMA,
        ],
        compiler_params=params(),
        cost_estimate=cost(6 * pairs, 4 << 20),
        name="attend",
    )(plan, turned_query, own_scores, own, far, near)
    weights, sends = outs[0], outs[1:]
    arrived = [exchange(sends[k], k) for k in range(n_dp - 1, 0, -1)] + [sends[0]]
    terms = jax.ShapeDtypeStruct((2 * block, kv_width), BF16)
    half = jax.ShapeDtypeStruct((block, kv_width), BF16)
    mark = jax.ShapeDtypeStruct((8, HEAD_DIM), F32)
    score_grads, d2, dk1, dv1 = pl.pallas_call(
        sent_kernel,
        out_shape=[jax.ShapeDtypeStruct(weights.shape, BF16), terms, half, half],
        in_specs=[VMEM] * 8,
        out_specs=[VMEM] * 4,
        compiler_params=params(),
        cost_estimate=cost(0, 0),
        name="sent_terms",
    )(query, grad, turned_grad, own_terms, own, far, near, weights)
    dq, d0, after_kept = pl.pallas_call(
        kept_kernel,
        out_shape=[
            jax.ShapeDtypeStruct((block, width), BF16),
            jax.ShapeDtypeStruct((2 * block, kv_width), F32),
            mark,
        ],
        in_specs=[VMEM] * 7,
        out_specs=[VMEM] * 3,
        compiler_params=params(),
        cost_estimate=cost(1073741824, 0),
        name="kept_terms",
    )(query, grad, own, far, near, weights, score_grads)
    dk1_in, dv1_in = swap(dk1), swap(dv1)
    d2_sum = pl.pallas_call(
        merge_kernel,
        out_shape=terms,
        in_specs=[VMEM] * 3,
        out_specs=VMEM,
        compiler_params=params(),
        cost_estimate=cost(0, 0),
        name="merge",
    )(d2, dk1_in, dv1_in)
    d2_even, d2_uneven = from_chip(d2_sum)
    routed_shape = jax.ShapeDtypeStruct((1, 1, n_dp, capacity, piece_len, width), BF16)
    routed = pl.pallas_call(
        functools.partial(early_kernel, n_dp),
        out_shape=routed_shape,
        in_specs=[HBM] * 3,
        out_specs=HBM,
        scratch_shapes=[pltpu.SemaphoreType.DMA((2,))],
        compiler_params=params(),
        cost_estimate=cost(2147483648, 0),
        name="place_early",
    )(after_kept, arrived[0], arrived[-1])
    routed, dk, dv = pl.pallas_call(
        functools.partial(finish_kernel, n_dp, n_ctx),
        out_shape=[routed_shape] + [jax.ShapeDtypeStruct((block, kv_width), BF16)] * 2,
        in_specs=[HBM] * (n_dp - 2) + [VMEM] * 5 + [HBM],
        out_specs=[HBM] * 3,
        input_output_aliases={n_dp + 3: 0},
        scratch_shapes=[
            pltpu.VMEM((2 * block, kv_width), BF16),
            pltpu.SemaphoreType.DMA((n_dp,)),
        ],
        compiler_params=params(),
        cost_estimate=cost(0, 1 << 20),
        name="finish",
    )(*arrived[1:-1], d2_uneven, d2_even, dk1_in, dv1_in, d0, *pinned(routed))
    return routed, dq[None], dk[None], dv[None]


def solution(mesh):
    rows = P("dp", "ctx", None)
    return jax.shard_map(
        on_device,
        mesh=mesh,
        in_specs=(rows, rows, rows, rows, P("dp", "ctx"), P("dp", "ctx")),
        out_specs=(P("dp", "ctx", None, None, None, None), rows, rows, rows),
        check_vma=False,
    )
```

```python
import functools
import math

import jax
import jax.numpy as jnp
from jax import lax
from jax.experimental import pallas as pl
from jax.experimental.pallas import tpu as pltpu
from jax.sharding import PartitionSpec as P

HEAD_DIM = 128
GROUP = 4
SEG_ROWS = 16
F32 = jnp.float32
BF16 = jnp.bfloat16
NEG = -1e30

NT = (((1,), (1,)), ((), ()))
NN = (((1,), (0,)), ((), ()))
TN = (((0,), (0,)), ((), ()))


def dot(a, b, dims):
    return lax.dot_general(a, b, dims, preferred_element_type=F32)


def stacked(ref, g):
    heads = [
        ref[:, (g * GROUP + h) * HEAD_DIM : (g * GROUP + h + 1) * HEAD_DIM] for h in range(GROUP)
    ]
    return jnp.concatenate(heads, axis=0)


def window(g, block, own_ref, far_ref, near_ref):
    cols = slice(g * HEAD_DIM, (g + 1) * HEAD_DIM)
    keys = (own_ref[0:block, cols], near_ref[0:block, cols], far_ref[0:block, cols])
    values = (
        own_ref[block : 2 * block, cols],
        near_ref[block : 2 * block, cols],
        far_ref[block : 2 * block, cols],
    )
    return keys, values


def triangle(block, copies):
    key_pos = lax.broadcasted_iota(jnp.int32, (block, copies * block), 0)
    query_pos = lax.broadcasted_iota(jnp.int32, (block, copies * block), 1)
    return key_pos <= lax.rem(query_pos, block)


def step_between(home, row, count):
    return home ^ row if count & (count - 1) == 0 else lax.rem(home - row + count, count)


def fwd_kernel(n_dp, home_hbm, qt_ref, s0_ref, own_ref, far_ref, near_ref, *rest):
    p_ref = rest[0]
    sends = rest[1 : 1 + n_dp]
    held, counts, filled, home_ref, sem = rest[1 + n_dp :]
    fetch = pltpu.make_async_copy(home_hbm, home_ref, sem)
    fetch.start()
    block = s0_ref.shape[1]
    column, row = lax.axis_index("ctx"), lax.axis_index("dp")
    pieces = home_ref.shape[1]
    piece_len = block // pieces
    capacity = sends[0].shape[0]
    held[pieces] = jnp.zeros(held.shape[1:], held.dtype)

    def seg_of(value):
        return value[2 * block : 2 * block + SEG_ROWS, 0:block].astype(F32)[0:1]

    seg_own, seg_near, seg_far = seg_of(own_ref), seg_of(near_ref), seg_of(far_ref)
    first = seg_own[:, 0:1]
    reach = jnp.where(column >= 1, jnp.sum((seg_near == first).astype(F32), axis=1, keepdims=True), 0.0)
    reach = reach + jnp.where(
        column >= 2, jnp.sum((seg_far == first).astype(F32), axis=1, keepdims=True), 0.0
    )
    key_pos = lax.broadcasted_iota(jnp.int32, (block, block), 0).astype(F32)
    tri = triangle(block, 1)
    seg_rows = jnp.broadcast_to(seg_own, (block, block))
    joined = seg_rows == first
    own_ok = seg_rows == seg_rows.T
    far_ok = (key_pos >= 2 * block - reach) & joined
    near_ok = (key_pos >= block - reach) & joined
    bias_x = jnp.where((tri & own_ok) | (~tri & far_ok), 0.0, NEG)
    bias_n = jnp.where(near_ok, 0.0, NEG)
    bias_x = jnp.concatenate([bias_x] * GROUP, axis=1)
    bias_n = jnp.concatenate([bias_n] * GROUP, axis=1)
    tri_g, lower = triangle(block, GROUP), lower_mask(block)
    scaling = math.log2(math.e) / math.sqrt(HEAD_DIM)

    for g in range(own_ref.shape[1] // HEAD_DIM):
        keys, values = window(g, block, own_ref, far_ref, near_ref)
        scores = dot(jnp.concatenate(keys[1:], axis=0), qt_ref[g], NN)
        s_x = jnp.where(tri_g, s0_ref[g], scores[block:]) * scaling + bias_x
        s_n = scores[0:block] * scaling + bias_n
        highest = jnp.max(jnp.maximum(s_x, s_n), axis=0, keepdims=True)
        e_x = jnp.exp2(s_x - highest)
        e_n = jnp.exp2(s_n - highest)
        inverse = 1.0 / jnp.sum(e_x + e_n, axis=0, keepdims=True)
        w_x = (e_x * inverse).astype(BF16)
        w_n = (e_n * inverse).astype(BF16)
        p_ref[g, 0:block] = w_x
        p_ref[g, block : 2 * block] = w_n
        w_0, w_2 = split(lower, w_x)
        weights = jnp.concatenate([w_0, w_n, w_2], axis=0)
        attended = dot(jnp.concatenate(values, axis=0), weights, TN).astype(BF16)
        for h in range(GROUP):
            cols = slice((g * GROUP + h) * HEAD_DIM, (g * GROUP + h + 1) * HEAD_DIM)
            tile = attended[:, h * block : (h + 1) * block].T
            held[0:pieces, :, cols] = tile.reshape(pieces, piece_len, HEAD_DIM)
    fetch.wait()
    for d in range(n_dp):
        counts[d] = 0
        for slot in range(capacity):
            filled[d * capacity + slot] = pieces
    for m in range(pieces):
        step = step_between(home_ref[0, m], row, n_dp)
        slot = counts[step]
        counts[step] = slot + 1
        filled[step * capacity + slot] = m
    for d in range(n_dp):
        for slot in range(capacity):
            sends[d][slot] = held[filled[d * capacity + slot]]


def split(lower, packed):
    own = packed * lower
    return own, packed - own


def lower_mask(block):
    return jnp.where(triangle(block, GROUP), 1.0, 0.0).astype(BF16)


def ahead_kernel(home_ref, q_ref, do_ref, own_ref, plan_ref, qt_ref, gt_ref, s0_ref, gw0_ref):
    plan_ref[...] = home_ref[...]
    block = q_ref.shape[0]
    for g in range(own_ref.shape[1] // HEAD_DIM):
        cols = slice(g * HEAD_DIM, (g + 1) * HEAD_DIM)
        for source, turned, product, rows in (
            (q_ref, qt_ref, s0_ref, slice(0, block)),
            (do_ref, gt_ref, gw0_ref, slice(block, 2 * block)),
        ):
            turned[g] = stacked(source, g).T
            product[g] = dot(own_ref[rows, cols], turned[g], NN)


def sent_kernel(q_ref, do_ref, gt_ref, gw0_ref, own_ref, far_ref, near_ref, p_ref, gs_ref, d2_ref, dk1_ref, dv1_ref):
    block = q_ref.shape[0]
    tri_g, lower = triangle(block, GROUP), lower_mask(block)
    scaling = 1.0 / math.sqrt(HEAD_DIM)
    for g in range(own_ref.shape[1] // HEAD_DIM):
        _, values = window(g, block, own_ref, far_ref, near_ref)
        queries, grads = stacked(q_ref, g), stacked(do_ref, g)
        w_xb = p_ref[g, 0:block]
        w_x = w_xb.astype(F32)
        w_n = p_ref[g, block : 2 * block]
        w_nf = w_n.astype(F32)
        score_terms = dot(jnp.concatenate(values[1:], axis=0), gt_ref[g], NN)
        gw_x = jnp.where(tri_g, gw0_ref[g], score_terms[block:])
        gw_n = score_terms[0:block]
        delta = jnp.sum(w_x * gw_x + w_nf * gw_n, axis=0, keepdims=True)
        gs_x = (w_x * (gw_x - delta) * scaling).astype(BF16)
        gs_n = (w_nf * (gw_n - delta) * scaling).astype(BF16)
        gs_ref[g, 0:block] = gs_x
        gs_ref[g, block : 2 * block] = gs_n
        _, gs_2 = split(lower, gs_x)
        _, w_2 = split(lower, w_xb)
        cols = slice(g * HEAD_DIM, (g + 1) * HEAD_DIM)
        dk = dot(jnp.concatenate([gs_n, gs_2], axis=0), queries, NN).astype(d2_ref.dtype)
        dv = dot(jnp.concatenate([w_n, w_2], axis=0), grads, NN).astype(d2_ref.dtype)
        dk1_ref[:, cols] = dk[0:block]
        dv1_ref[:, cols] = dv[0:block]
        d2_ref[0:block, cols] = dk[block:]
        d2_ref[block : 2 * block, cols] = dv[block:]


def kept_kernel(q_ref, do_ref, own_ref, far_ref, near_ref, p_ref, gs_ref, dq_ref, d0_ref, mark_ref):
    mark_ref[...] = jnp.zeros_like(mark_ref)
    block = q_ref.shape[0]
    lower = lower_mask(block)
    for g in range(own_ref.shape[1] // HEAD_DIM):
        keys, _ = window(g, block, own_ref, far_ref, near_ref)
        queries, grads = stacked(q_ref, g), stacked(do_ref, g)
        gs_0, gs_2 = split(lower, gs_ref[g, 0:block])
        w_0, _ = split(lower, p_ref[g, 0:block])
        gs_n = gs_ref[g, block : 2 * block]
        cols = slice(g * HEAD_DIM, (g + 1) * HEAD_DIM)
        d0_ref[0:block, cols] = dot(gs_0, queries, NN)
        d0_ref[block : 2 * block, cols] = dot(w_0, grads, NN)
        dq = dot(jnp.concatenate([gs_0, gs_n, gs_2], axis=0), jnp.concatenate(keys, axis=0), TN)
        for h in range(GROUP):
            heads = slice((g * GROUP + h) * HEAD_DIM, (g * GROUP + h + 1) * HEAD_DIM)
            dq_ref[:, heads] = dq[h * block : (h + 1) * block].astype(dq_ref.dtype)


def prep_kernel(seg_hbm, k_hbm, v_hbm, own_ref, seg_ref, sems):
    block = k_hbm.shape[0]
    copies = [
        pltpu.make_async_copy(seg_hbm, seg_ref, sems.at[0]),
        pltpu.make_async_copy(k_hbm, own_ref.at[0:block], sems.at[1]),
        pltpu.make_async_copy(v_hbm, own_ref.at[block : 2 * block], sems.at[2]),
    ]
    for copy in copies:
        copy.start()
    tail = slice(2 * block, 2 * block + SEG_ROWS)
    own_ref[tail, block:] = jnp.zeros((SEG_ROWS, own_ref.shape[1] - block), BF16)
    copies[0].wait()
    ids = jnp.broadcast_to(seg_ref[...].astype(F32), (SEG_ROWS, block))
    own_ref[tail, 0:block] = ids.astype(BF16)
    for copy in copies[1:]:
        copy.wait()


def merge_kernel(d2_ref, dk1_ref, dv1_ref, out_ref):
    block = dk1_ref.shape[0]
    odd = lax.rem(lax.axis_index("ctx"), 2) == 1
    for part, d1_ref in enumerate((dk1_ref, dv1_ref)):
        rows = slice(part * block, (part + 1) * block)
        other = jnp.where(odd, d1_ref[...].astype(F32), 0.0)
        out_ref[rows] = (d2_ref[rows].astype(F32) + other).astype(out_ref.dtype)


def source_row(row, step, count):
    return row ^ step if count & (count - 1) == 0 else lax.rem(row - step + count, count)


def early_kernel(n_dp, kept_ref, far_ref, own_ref, out_ref, sems):
    row = lax.axis_index("dp")
    copies = [
        pltpu.make_async_copy(own_ref, out_ref.at[0, 0, row], sems.at[0]),
        pltpu.make_async_copy(
            far_ref, out_ref.at[0, 0, source_row(row, n_dp - 1, n_dp)], sems.at[1]
        ),
    ]
    for copy in copies:
        copy.start()
    for copy in copies:
        copy.wait()


def finish_kernel(n_dp, n_ctx, *rest):
    pieces, rest = rest[: n_dp - 2], rest[n_dp - 2 :]
    uneven_ref, even_ref, dk1_ref, dv1_ref, d0_ref, _, out_ref, dk_ref, dv_ref, total_ref, sems = rest
    row, column = lax.axis_index("dp"), lax.axis_index("ctx")
    block = dk_ref.shape[0]
    copies = []
    for i in range(n_dp - 2):
        target = out_ref.at[0, 0, source_row(row, n_dp - 2 - i, n_dp)]
        copies.append(pltpu.make_async_copy(pieces[i], target, sems.at[i]))
        copies[-1].start()
    for part, (d1_ref, target) in enumerate(((dk1_ref, dk_ref), (dv1_ref, dv_ref))):
        rows = slice(part * block, (part + 1) * block)
        total = d0_ref[rows]
        total = total + jnp.where(lax.rem(column, 2) == 0, d1_ref[...].astype(F32), 0.0)
        d2 = jnp.where(lax.rem(column // 2, 2) == 0, even_ref[rows], uneven_ref[rows])
        total = total + jnp.where(column + 2 < n_ctx, d2.astype(F32), 0.0)
        total_ref[rows] = total.astype(total_ref.dtype)
        copies.append(pltpu.make_async_copy(total_ref.at[rows], target, sems.at[n_dp - 2 + part]))
        copies[-1].start()
    for copy in copies:
        copy.wait()


VMEM = pl.BlockSpec(memory_space=pltpu.VMEM)
HBM = pl.BlockSpec(memory_space=pl.ANY)


def params(kib=32 * 1024):
    return pltpu.CompilerParams(vmem_limit_bytes=kib * 1024)


def cost(flops, nbytes):
    return pl.CostEstimate(flops=flops, bytes_accessed=nbytes, transcendentals=0)


def pinned(*arrays):
    return [pltpu.with_memory_space_constraint(array, pltpu.HBM) for array in arrays]


def swap(value):
    count = lax.axis_size("ctx")
    return lax.ppermute(value, "ctx", [(i, i ^ 1) for i in range(count)])


def from_chip(value, colours):
    count = lax.axis_size("ctx")

    def pairs(colour):
        found = []
        for i in range(count):
            chip, core = i // 2, i % 2
            other = chip + 1 if chip % colours == colour else chip - 1 if (chip - 1) % colours == colour else -1
            found.append((i, 2 * other + core if 0 <= other < count // 2 else i ^ 1))
        return found

    return [lax.ppermute(value, "ctx", pairs(colour)) for colour in range(colours)]


def exchange(value, k):
    count = lax.axis_size("dp")
    if count & (count - 1) == 0:
        pairs = [(i, i ^ k) for i in range(count)]
    else:
        pairs = [(i, (i + k) % count) for i in range(count)]
    return lax.ppermute(value, "dp", pairs)


def on_device(query_rows, key_rows, value_rows, out_grad, segment_ids, home_rows):
    n_dp, n_ctx = lax.axis_size("dp"), lax.axis_size("ctx")
    query, grad = query_rows[0], out_grad[0]
    block, width = query.shape
    kv_width = key_rows.shape[2]
    heads = kv_width // HEAD_DIM
    pieces = home_rows.shape[1]
    capacity = max(2, 2 * pieces // n_dp)
    piece_len = block // pieces
    column = lax.axis_index("ctx")
    own = pl.pallas_call(
        prep_kernel,
        out_shape=jax.ShapeDtypeStruct((2 * block + SEG_ROWS, kv_width), BF16),
        in_specs=[HBM] * 3,
        out_specs=VMEM,
        scratch_shapes=[pltpu.VMEM((1, block), jnp.int32), pltpu.SemaphoreType.DMA((3,))],
        compiler_params=params(),
        cost_estimate=cost(0, 1 << 19),
        name="bundle",
    )(*pinned(segment_ids, key_rows[0], value_rows[0]))
    moved = from_chip(own, 3)
    colour = lax.rem(column // 2 + 2, 3)
    far = jnp.where(colour == 2, moved[2], jnp.where(colour == 1, moved[1], moved[0]))
    beside = swap(own)
    near = jnp.where(lax.rem(column, 2) == 0, swap(far), beside)

    pairs = 2 * block * block * GROUP * heads * HEAD_DIM
    turned = jax.ShapeDtypeStruct((heads, HEAD_DIM, GROUP * block), BF16)
    product = jax.ShapeDtypeStruct((heads, block, GROUP * block), F32)
    plan, turned_query, turned_grad, own_scores, own_terms = pl.pallas_call(
        ahead_kernel,
        out_shape=[
            jax.ShapeDtypeStruct(home_rows.shape, jnp.int32), turned, turned, product, product
        ],
        in_specs=[VMEM] * 4,
        out_specs=[VMEM] * 5,
        compiler_params=params(),
        cost_estimate=cost(2 * pairs, 4 << 20),
        name="ahead",
    )(home_rows, query, grad, own)
    outs = pl.pallas_call(
        functools.partial(fwd_kernel, n_dp),
        out_shape=[jax.ShapeDtypeStruct((heads, 2 * block, GROUP * block), BF16)]
        + [jax.ShapeDtypeStruct((capacity, piece_len, width), BF16)] * n_dp,
        in_specs=[HBM] + [VMEM] * 5,
        out_specs=[VMEM] * (1 + n_dp),
        scratch_shapes=[
            pltpu.VMEM((pieces + 1, piece_len, width), BF16),
            pltpu.SMEM((n_dp,), jnp.int32),
            pltpu.SMEM((n_dp * capacity,), jnp.int32),
            pltpu.SMEM((1, pieces), jnp.int32),
            pltpu.SemaphoreType.DMA,
        ],
        compiler_params=params(),
        cost_estimate=cost(6 * pairs, 4 << 20),
        name="attend",
    )(plan, turned_query, own_scores, own, far, near)
    weights, sends = outs[0], outs[1:]
    arrived = [exchange(sends[k], k) for k in range(n_dp - 1, 0, -1)] + [sends[0]]
    terms = jax.ShapeDtypeStruct((2 * block, kv_width), BF16)
    half = jax.ShapeDtypeStruct((block, kv_width), BF16)
    mark = jax.ShapeDtypeStruct((8, HEAD_DIM), F32)
    score_grads, d2, dk1, dv1 = pl.pallas_call(
        sent_kernel,
        out_shape=[jax.ShapeDtypeStruct(weights.shape, BF16), terms, half, half],
        in_specs=[VMEM] * 8,
        out_specs=[VMEM] * 4,
        compiler_params=params(),
        cost_estimate=cost(0, 0),
        name="sent_terms",
    )(query, grad, turned_grad, own_terms, own, far, near, weights)
    dq, d0, after_kept = pl.pallas_call(
        kept_kernel,
        out_shape=[
            jax.ShapeDtypeStruct((block, width), BF16),
            jax.ShapeDtypeStruct((2 * block, kv_width), F32),
            mark,
        ],
        in_specs=[VMEM] * 7,
        out_specs=[VMEM] * 3,
        compiler_params=params(),
        cost_estimate=cost(1073741824, 0),
        name="kept_terms",
    )(query, grad, own, far, near, weights, score_grads)
    dk1_in, dv1_in = swap(dk1), swap(dv1)
    d2_sum = pl.pallas_call(
        merge_kernel,
        out_shape=terms,
        in_specs=[VMEM] * 3,
        out_specs=VMEM,
        compiler_params=params(),
        cost_estimate=cost(0, 0),
        name="merge",
    )(d2, dk1_in, dv1_in)
    d2_even, d2_uneven = from_chip(d2_sum, 2)
    routed_shape = jax.ShapeDtypeStruct((1, 1, n_dp, capacity, piece_len, width), BF16)
    routed = pl.pallas_call(
        functools.partial(early_kernel, n_dp),
        out_shape=routed_shape,
        in_specs=[HBM] * 3,
        out_specs=HBM,
        scratch_shapes=[pltpu.SemaphoreType.DMA((2,))],
        compiler_params=params(),
        cost_estimate=cost(2147483648, 0),
        name="place_early",
    )(after_kept, arrived[0], arrived[-1])
    routed, dk, dv = pl.pallas_call(
        functools.partial(finish_kernel, n_dp, n_ctx),
        out_shape=[routed_shape] + [jax.ShapeDtypeStruct((block, kv_width), BF16)] * 2,
        in_specs=[HBM] * (n_dp - 2) + [VMEM] * 5 + [HBM],
        out_specs=[HBM] * 3,
        input_output_aliases={n_dp + 3: 0},
        scratch_shapes=[
            pltpu.VMEM((2 * block, kv_width), BF16),
            pltpu.SemaphoreType.DMA((n_dp,)),
        ],
        compiler_params=params(),
        cost_estimate=cost(0, 1 << 20),
        name="finish",
    )(*arrived[1:-1], d2_uneven, d2_even, dk1_in, dv1_in, d0, *pinned(routed))
    return routed, dq[None], dk[None], dv[None]


def solution(mesh):
    rows = P("dp", "ctx", None)
    return jax.shard_map(
        on_device,
        mesh=mesh,
        in_specs=(rows, rows, rows, rows, P("dp", "ctx"), P("dp", "ctx")),
        out_specs=(P("dp", "ctx", None, None, None, None), rows, rows, rows),
        check_vma=False,
    )
```

```python
import functools
import math

import jax
import jax.numpy as jnp
from jax import lax
from jax.experimental import pallas as pl
from jax.experimental.pallas import tpu as pltpu
from jax.sharding import PartitionSpec as P

HEAD_DIM = 128
GROUP = 4
SEG_ROWS = 16
F32 = jnp.float32
BF16 = jnp.bfloat16
NEG = -1e30

NT = (((1,), (1,)), ((), ()))
NN = (((1,), (0,)), ((), ()))
TN = (((0,), (0,)), ((), ()))


def dot(a, b, dims):
    return lax.dot_general(a, b, dims, preferred_element_type=F32)


def stacked(ref, g):
    heads = [
        ref[:, (g * GROUP + h) * HEAD_DIM : (g * GROUP + h + 1) * HEAD_DIM] for h in range(GROUP)
    ]
    return jnp.concatenate(heads, axis=0)


def head_blocks(g, block, own_ref, far_ref, near_ref):
    cols = slice(g * HEAD_DIM, (g + 1) * HEAD_DIM)
    return [ref[0:block, cols] for ref in (own_ref, near_ref, far_ref)]


def triangle(block, copies):
    key_pos = lax.broadcasted_iota(jnp.int32, (block, copies * block), 0)
    query_pos = lax.broadcasted_iota(jnp.int32, (block, copies * block), 1)
    return key_pos <= lax.rem(query_pos, block)


def step_between(home, row, count):
    return home ^ row if count & (count - 1) == 0 else lax.rem(home - row + count, count)


def weights_kernel(qt_ref, s0_ref, own_ref, far_ref, near_ref, p_ref):
    block = s0_ref.shape[1]
    column = lax.axis_index("ctx")

    def seg_of(ref):
        return ref[block : block + SEG_ROWS, 0:block].astype(F32)[0:1]

    seg_own, seg_near, seg_far = seg_of(own_ref), seg_of(near_ref), seg_of(far_ref)
    first = seg_own[:, 0:1]
    reach = jnp.where(column >= 1, jnp.sum((seg_near == first).astype(F32), axis=1, keepdims=True), 0.0)
    reach = reach + jnp.where(
        column >= 2, jnp.sum((seg_far == first).astype(F32), axis=1, keepdims=True), 0.0
    )
    key_pos = lax.broadcasted_iota(jnp.int32, (block, block), 0).astype(F32)
    tri = triangle(block, 1)
    seg_rows = jnp.broadcast_to(seg_own, (block, block))
    joined = seg_rows == first
    own_ok = seg_rows == seg_rows.T
    far_ok = (key_pos >= 2 * block - reach) & joined
    near_ok = (key_pos >= block - reach) & joined
    bias_x = jnp.where((tri & own_ok) | (~tri & far_ok), 0.0, NEG)
    bias_n = jnp.where(near_ok, 0.0, NEG)
    bias_x = jnp.concatenate([bias_x] * GROUP, axis=1)
    bias_n = jnp.concatenate([bias_n] * GROUP, axis=1)
    tri_g = triangle(block, GROUP)
    scaling = math.log2(math.e) / math.sqrt(HEAD_DIM)
    for g in range(qt_ref.shape[0]):
        keys = head_blocks(g, block, own_ref, far_ref, near_ref)
        scores = dot(jnp.concatenate(keys[1:], axis=0), qt_ref[g], NN)
        s_x = jnp.where(tri_g, s0_ref[g], scores[block:]) * scaling + bias_x
        s_n = scores[0:block] * scaling + bias_n
        highest = jnp.max(jnp.maximum(s_x, s_n), axis=0, keepdims=True)
        e_x = jnp.exp2(s_x - highest)
        e_n = jnp.exp2(s_n - highest)
        inverse = 1.0 / jnp.sum(e_x + e_n, axis=0, keepdims=True)
        p_ref[g, 0:block] = (e_x * inverse).astype(BF16)
        p_ref[g, block : 2 * block] = (e_n * inverse).astype(BF16)


def attend_kernel(n_dp, home_hbm, p_ref, own_ref, far_ref, near_ref, *rest):
    sends, (held, counts, filled, home_ref, sem) = rest[:n_dp], rest[n_dp:]
    fetch = pltpu.make_async_copy(home_hbm, home_ref, sem)
    fetch.start()
    block = own_ref.shape[0]
    row = lax.axis_index("dp")
    pieces = home_ref.shape[1]
    piece_len = block // pieces
    capacity = sends[0].shape[0]
    held[pieces] = jnp.zeros(held.shape[1:], held.dtype)
    lower = lower_mask(block)
    for g in range(p_ref.shape[0]):
        values = head_blocks(g, block, own_ref, far_ref, near_ref)
        w_0, w_2 = split(lower, p_ref[g, 0:block])
        weights = jnp.concatenate([w_0, p_ref[g, block : 2 * block], w_2], axis=0)
        attended = dot(jnp.concatenate(values, axis=0), weights, TN).astype(BF16)
        for h in range(GROUP):
            cols = slice((g * GROUP + h) * HEAD_DIM, (g * GROUP + h + 1) * HEAD_DIM)
            tile = attended[:, h * block : (h + 1) * block].T
            held[0:pieces, :, cols] = tile.reshape(pieces, piece_len, HEAD_DIM)
    fetch.wait()
    for d in range(n_dp):
        counts[d] = 0
        for slot in range(capacity):
            filled[d * capacity + slot] = pieces
    for m in range(pieces):
        step = step_between(home_ref[0, m], row, n_dp)
        slot = counts[step]
        counts[step] = slot + 1
        filled[step * capacity + slot] = m
    for d in range(n_dp - 1, -1, -1):
        for slot in range(capacity):
            sends[d][slot] = held[filled[d * capacity + slot]]


def split(lower, packed):
    own = packed * lower
    return own, packed - own


def lower_mask(block):
    return jnp.where(triangle(block, GROUP), 1.0, 0.0).astype(BF16)


def ahead_kernel(
    home_hbm, q_hbm, do_hbm, v_hbm, key_ref,
    plan_ref, qt_ref, gt_ref, s0_ref, gw0_ref, q_ref, do_ref, v_ref, sems,
):
    pairs = ((q_hbm, q_ref), (do_hbm, do_ref), (v_hbm, v_ref), (home_hbm, plan_ref))
    copies = [pltpu.make_async_copy(*pair, sems.at[i]) for i, pair in enumerate(pairs)]
    for copy in copies:
        copy.start()
    block = q_ref.shape[0]
    for source, own_ref, turned, product, waits in (
        (q_ref, key_ref, qt_ref, s0_ref, copies[:1]),
        (do_ref, v_ref, gt_ref, gw0_ref, copies[1:]),
    ):
        for copy in waits:
            copy.wait()
        for g in range(qt_ref.shape[0]):
            turned[g] = stacked(source, g).T
            product[g] = dot(own_ref[0:block, g * HEAD_DIM : (g + 1) * HEAD_DIM], turned[g], NN)


def sent_kernel(q_ref, do_ref, gt_ref, gw0_ref, own_ref, far_ref, near_ref, p_ref, gs_ref, d2_ref, dk1_ref, dv1_ref):
    block = q_ref.shape[0]
    tri_g, lower = triangle(block, GROUP), lower_mask(block)
    scaling = 1.0 / math.sqrt(HEAD_DIM)
    for g in range(own_ref.shape[1] // HEAD_DIM):
        values = head_blocks(g, block, own_ref, far_ref, near_ref)
        queries, grads = stacked(q_ref, g), stacked(do_ref, g)
        w_xb = p_ref[g, 0:block]
        w_x = w_xb.astype(F32)
        w_n = p_ref[g, block : 2 * block]
        w_nf = w_n.astype(F32)
        score_terms = dot(jnp.concatenate(values[1:], axis=0), gt_ref[g], NN)
        gw_x = jnp.where(tri_g, gw0_ref[g], score_terms[block:])
        gw_n = score_terms[0:block]
        delta = jnp.sum(w_x * gw_x + w_nf * gw_n, axis=0, keepdims=True)
        gs_x = (w_x * (gw_x - delta) * scaling).astype(BF16)
        gs_n = (w_nf * (gw_n - delta) * scaling).astype(BF16)
        gs_ref[g, 0:block] = gs_x
        gs_ref[g, block : 2 * block] = gs_n
        _, gs_2 = split(lower, gs_x)
        _, w_2 = split(lower, w_xb)
        cols = slice(g * HEAD_DIM, (g + 1) * HEAD_DIM)
        dk = dot(jnp.concatenate([gs_n, gs_2], axis=0), queries, NN).astype(d2_ref.dtype)
        dv = dot(jnp.concatenate([w_n, w_2], axis=0), grads, NN).astype(d2_ref.dtype)
        dk1_ref[:, cols] = dk[0:block]
        dv1_ref[:, cols] = dv[0:block]
        d2_ref[0:block, cols] = dk[block:]
        d2_ref[block : 2 * block, cols] = dv[block:]


def kept_kernel(q_ref, do_ref, own_ref, far_ref, near_ref, p_ref, gs_ref, dq_ref, d0_ref, mark_ref):
    mark_ref[...] = jnp.zeros_like(mark_ref)
    block = q_ref.shape[0]
    lower = lower_mask(block)
    for g in range(own_ref.shape[1] // HEAD_DIM):
        keys = head_blocks(g, block, own_ref, far_ref, near_ref)
        queries, grads = stacked(q_ref, g), stacked(do_ref, g)
        gs_0, gs_2 = split(lower, gs_ref[g, 0:block])
        w_0, _ = split(lower, p_ref[g, 0:block])
        gs_n = gs_ref[g, block : 2 * block]
        cols = slice(g * HEAD_DIM, (g + 1) * HEAD_DIM)
        d0_ref[0:block, cols] = dot(gs_0, queries, NN)
        d0_ref[block : 2 * block, cols] = dot(w_0, grads, NN)
        dq = dot(jnp.concatenate([gs_0, gs_n, gs_2], axis=0), jnp.concatenate(keys, axis=0), TN)
        for h in range(GROUP):
            heads = slice((g * GROUP + h) * HEAD_DIM, (g * GROUP + h + 1) * HEAD_DIM)
            dq_ref[:, heads] = dq[h * block : (h + 1) * block].astype(dq_ref.dtype)


def bundle_kernel(seg_hbm, k_hbm, own_ref, seg_ref, sems):
    block = k_hbm.shape[0]
    copies = [
        pltpu.make_async_copy(seg_hbm, seg_ref, sems.at[0]),
        pltpu.make_async_copy(k_hbm, own_ref.at[0:block], sems.at[1]),
    ]
    for copy in copies:
        copy.start()
    tail = slice(block, block + SEG_ROWS)
    own_ref[tail, block:] = jnp.zeros((SEG_ROWS, own_ref.shape[1] - block), BF16)
    copies[0].wait()
    ids = jnp.broadcast_to(seg_ref[...].astype(F32), (SEG_ROWS, block))
    own_ref[tail, 0:block] = ids.astype(BF16)
    copies[1].wait()


def pick_kernel(colours, own_ref, *rest):
    moved_refs, (_, out_ref, crossing_ref) = rest[:colours], rest[colours:]
    chip, core = lax.axis_index("ctx") // 2, lax.rem(lax.axis_index("ctx"), 2)
    colour = lax.rem(chip + colours - 1, colours)
    picked = moved_refs[0][...]
    for i in range(1, colours):
        picked = jnp.where(colour == colours - 1 - i, moved_refs[i][...], picked)
    out_ref[...] = picked
    crossing_ref[...] = jnp.where(core == 0, own_ref[...], picked)


def merge_kernel(d2_ref, dk1_ref, dv1_ref, out_ref):
    block = dk1_ref.shape[0]
    odd = lax.rem(lax.axis_index("ctx"), 2) == 1
    for part, d1_ref in enumerate((dk1_ref, dv1_ref)):
        rows = slice(part * block, (part + 1) * block)
        other = jnp.where(odd, d1_ref[...].astype(F32), 0.0)
        out_ref[rows] = (d2_ref[rows].astype(F32) + other).astype(out_ref.dtype)


def source_row(row, step, count):
    return row ^ step if count & (count - 1) == 0 else lax.rem(row - step + count, count)


def early_kernel(n_dp, kept_ref, far_ref, own_ref, out_ref, sems):
    row = lax.axis_index("dp")
    copies = [
        pltpu.make_async_copy(own_ref, out_ref.at[0, 0, row], sems.at[0]),
        pltpu.make_async_copy(
            far_ref, out_ref.at[0, 0, source_row(row, n_dp - 1, n_dp)], sems.at[1]
        ),
    ]
    for copy in copies:
        copy.start()
    for copy in copies:
        copy.wait()


def finish_kernel(n_dp, n_ctx, *rest):
    pieces, rest = rest[: n_dp - 2], rest[n_dp - 2 :]
    uneven_ref, even_ref, dk1_ref, dv1_ref, d0_ref, _, out_ref, dk_ref, dv_ref, total_ref, sems = rest
    row, column = lax.axis_index("dp"), lax.axis_index("ctx")
    block = dk_ref.shape[0]
    copies = []
    for i in range(n_dp - 2):
        target = out_ref.at[0, 0, source_row(row, n_dp - 2 - i, n_dp)]
        copies.append(pltpu.make_async_copy(pieces[i], target, sems.at[i]))
        copies[-1].start()
    for part, (d1_ref, target) in enumerate(((dk1_ref, dk_ref), (dv1_ref, dv_ref))):
        rows = slice(part * block, (part + 1) * block)
        total = d0_ref[rows]
        total = total + jnp.where(lax.rem(column, 2) == 0, d1_ref[...].astype(F32), 0.0)
        d2 = jnp.where(lax.rem(column // 2, 2) == 0, even_ref[rows], uneven_ref[rows])
        total = total + jnp.where(column + 2 < n_ctx, d2.astype(F32), 0.0)
        total_ref[rows] = total.astype(total_ref.dtype)
        copies.append(pltpu.make_async_copy(total_ref.at[rows], target, sems.at[n_dp - 2 + part]))
        copies[-1].start()
    for copy in copies:
        copy.wait()


VMEM = pl.BlockSpec(memory_space=pltpu.VMEM)
HBM = pl.BlockSpec(memory_space=pl.ANY)


def params(kib=32 * 1024):
    return pltpu.CompilerParams(vmem_limit_bytes=kib * 1024)


def cost(flops, nbytes):
    return pl.CostEstimate(flops=flops, bytes_accessed=nbytes, transcendentals=0)


def pinned(*arrays):
    return [pltpu.with_memory_space_constraint(array, pltpu.HBM) for array in arrays]


def swap(value):
    count = lax.axis_size("ctx")
    return lax.ppermute(value, "ctx", [(i, i ^ 1) for i in range(count)])


def from_chip(value, colours):
    count = lax.axis_size("ctx")

    def pairs(colour):
        found = []
        for i in range(count):
            chip, core = i // 2, i % 2
            other = chip + 1 if chip % colours == colour else chip - 1 if (chip - 1) % colours == colour else -1
            found.append((i, 2 * other + core if 0 <= other < count // 2 else i ^ 1))
        return found

    return [lax.ppermute(value, "ctx", pairs(colour)) for colour in range(colours)]


def exchange(value, k):
    count = lax.axis_size("dp")
    if count & (count - 1) == 0:
        pairs = [(i, i ^ k) for i in range(count)]
    else:
        pairs = [(i, (i + k) % count) for i in range(count)]
    return lax.ppermute(value, "dp", pairs)


def on_device(query_rows, key_rows, value_rows, out_grad, segment_ids, home_rows):
    n_dp, n_ctx = lax.axis_size("dp"), lax.axis_size("ctx")
    query, grad = query_rows[0], out_grad[0]
    block, width = query.shape
    kv_width = key_rows.shape[2]
    heads = kv_width // HEAD_DIM
    pieces = home_rows.shape[1]
    capacity = max(2, 2 * pieces // n_dp)
    piece_len = block // pieces
    column = lax.axis_index("ctx")
    keys = pl.pallas_call(
        bundle_kernel,
        out_shape=jax.ShapeDtypeStruct((block + SEG_ROWS, kv_width), BF16),
        in_specs=[HBM] * 2,
        out_specs=VMEM,
        scratch_shapes=[pltpu.VMEM((1, block), jnp.int32), pltpu.SemaphoreType.DMA((2,))],
        compiler_params=params(),
        cost_estimate=cost(0, 1 << 19),
        name="bundle",
    )(*pinned(segment_ids, key_rows[0]))
    values = value_rows[0]
    moved_keys, moved_values = from_chip(keys, 3), from_chip(values, 2)

    turned = jax.ShapeDtypeStruct((heads, HEAD_DIM, GROUP * block), BF16)
    product = jax.ShapeDtypeStruct((heads, block, GROUP * block), F32)
    plan, turned_query, turned_grad, own_scores, own_terms, query, grad, own_values = pl.pallas_call(
        ahead_kernel,
        out_shape=[
            jax.ShapeDtypeStruct(home_rows.shape, jnp.int32), turned, turned, product, product,
            jax.ShapeDtypeStruct(query.shape, BF16), jax.ShapeDtypeStruct(grad.shape, BF16),
            jax.ShapeDtypeStruct(values.shape, BF16),
        ],
        in_specs=[HBM] * 4 + [VMEM],
        out_specs=[VMEM] * 8,
        scratch_shapes=[pltpu.SemaphoreType.DMA((4,))],
        compiler_params=params(),
        cost_estimate=cost(0, 0),
        name="ahead",
    )(*pinned(home_rows, query, grad, values), keys)
    far_keys, crossing = pl.pallas_call(
        functools.partial(pick_kernel, len(moved_keys)),
        out_shape=[jax.ShapeDtypeStruct(keys.shape, BF16)] * 2,
        in_specs=[VMEM] * (1 + len(moved_keys)) + [HBM],
        out_specs=[VMEM] * 2,
        compiler_params=params(),
        cost_estimate=cost(0, 0),
        name="pick_keys",
    )(keys, *moved_keys[::-1], plan)
    near_keys = swap(crossing)
    weights = pl.pallas_call(
        weights_kernel,
        out_shape=jax.ShapeDtypeStruct((heads, 2 * block, GROUP * block), BF16),
        in_specs=[VMEM] * 5,
        out_specs=VMEM,
        compiler_params=params(),
        cost_estimate=cost(0, 0),
        name="weights",
    )(turned_query, own_scores, keys, far_keys, near_keys)
    far_values, crossing = pl.pallas_call(
        functools.partial(pick_kernel, len(moved_values)),
        out_shape=[jax.ShapeDtypeStruct(values.shape, BF16)] * 2,
        in_specs=[VMEM] * (1 + len(moved_values)) + [HBM],
        out_specs=[VMEM] * 2,
        compiler_params=params(),
        cost_estimate=cost(0, 0),
        name="pick_values",
    )(own_values, *moved_values[::-1], plan)
    near_values = swap(crossing)
    sends = pl.pallas_call(
        functools.partial(attend_kernel, n_dp),
        out_shape=[jax.ShapeDtypeStruct((capacity, piece_len, width), BF16)] * n_dp,
        in_specs=[HBM] + [VMEM] * 4,
        out_specs=[VMEM] * n_dp,
        scratch_shapes=[
            pltpu.VMEM((pieces + 1, piece_len, width), BF16),
            pltpu.SMEM((n_dp,), jnp.int32),
            pltpu.SMEM((n_dp * capacity,), jnp.int32),
            pltpu.SMEM((1, pieces), jnp.int32),
            pltpu.SemaphoreType.DMA,
        ],
        compiler_params=params(),
        cost_estimate=cost(0, 0),
        name="attend",
    )(plan, weights, own_values, far_values, near_values)
    arrived = [exchange(sends[k], k) for k in range(n_dp - 1, 0, -1)] + [sends[0]]
    terms = jax.ShapeDtypeStruct((2 * block, kv_width), BF16)
    half = jax.ShapeDtypeStruct((block, kv_width), BF16)
    mark = jax.ShapeDtypeStruct((8, HEAD_DIM), F32)
    score_grads, d2, dk1, dv1 = pl.pallas_call(
        sent_kernel,
        out_shape=[jax.ShapeDtypeStruct(weights.shape, BF16), terms, half, half],
        in_specs=[VMEM] * 8,
        out_specs=[VMEM] * 4,
        compiler_params=params(),
        cost_estimate=cost(0, 0),
        name="sent_terms",
    )(query, grad, turned_grad, own_terms, own_values, far_values, near_values, weights)
    dq, d0, after_kept = pl.pallas_call(
        kept_kernel,
        out_shape=[
            jax.ShapeDtypeStruct((block, width), BF16),
            jax.ShapeDtypeStruct((2 * block, kv_width), F32),
            mark,
        ],
        in_specs=[VMEM] * 7,
        out_specs=[VMEM] * 3,
        compiler_params=params(),
        cost_estimate=cost(1073741824, 0),
        name="kept_terms",
    )(query, grad, keys, far_keys, near_keys, weights, score_grads)
    dk1_in, dv1_in = swap(dk1), swap(dv1)
    d2_sum = pl.pallas_call(
        merge_kernel,
        out_shape=terms,
        in_specs=[VMEM] * 3,
        out_specs=VMEM,
        compiler_params=params(),
        cost_estimate=cost(0, 0),
        name="merge",
    )(d2, dk1_in, dv1_in)
    d2_even, d2_uneven = from_chip(d2_sum, 2)
    routed_shape = jax.ShapeDtypeStruct((1, 1, n_dp, capacity, piece_len, width), BF16)
    routed = pl.pallas_call(
        functools.partial(early_kernel, n_dp),
        out_shape=routed_shape,
        in_specs=[HBM] * 3,
        out_specs=HBM,
        scratch_shapes=[pltpu.SemaphoreType.DMA((2,))],
        compiler_params=params(),
        cost_estimate=cost(2147483648, 0),
        name="place_early",
    )(after_kept, arrived[0], arrived[-1])
    routed, dk, dv = pl.pallas_call(
        functools.partial(finish_kernel, n_dp, n_ctx),
        out_shape=[routed_shape] + [jax.ShapeDtypeStruct((block, kv_width), BF16)] * 2,
        in_specs=[HBM] * (n_dp - 2) + [VMEM] * 5 + [HBM],
        out_specs=[HBM] * 3,
        input_output_aliases={n_dp + 3: 0},
        scratch_shapes=[
            pltpu.VMEM((2 * block, kv_width), BF16),
            pltpu.SemaphoreType.DMA((n_dp,)),
        ],
        compiler_params=params(),
        cost_estimate=cost(0, 1 << 20),
        name="finish",
    )(*arrived[1:-1], d2_uneven, d2_even, dk1_in, dv1_in, d0, *pinned(routed))
    return routed, dq[None], dk[None], dv[None]


def solution(mesh):
    rows = P("dp", "ctx", None)
    return jax.shard_map(
        on_device,
        mesh=mesh,
        in_specs=(rows, rows, rows, rows, P("dp", "ctx"), P("dp", "ctx")),
        out_specs=(P("dp", "ctx", None, None, None, None), rows, rows, rows),
        check_vma=False,
    )
```

```python
import functools
import math

import jax
import jax.numpy as jnp
from jax import lax
from jax.experimental import pallas as pl
from jax.experimental.pallas import tpu as pltpu
from jax.sharding import PartitionSpec as P

HEAD_DIM = 128
GROUP = 4
SEG_ROWS = 16
F32 = jnp.float32
BF16 = jnp.bfloat16
NEG = -1e30

NT = (((1,), (1,)), ((), ()))
NN = (((1,), (0,)), ((), ()))
TN = (((0,), (0,)), ((), ()))


def dot(a, b, dims):
    return lax.dot_general(a, b, dims, preferred_element_type=F32)


def stacked(ref, g):
    heads = [
        ref[:, (g * GROUP + h) * HEAD_DIM : (g * GROUP + h + 1) * HEAD_DIM] for h in range(GROUP)
    ]
    return jnp.concatenate(heads, axis=0)


def head_blocks(g, block, own_ref, far_ref, near_ref):
    cols = slice(g * HEAD_DIM, (g + 1) * HEAD_DIM)
    return [ref[0:block, cols] for ref in (own_ref, near_ref, far_ref)]


def triangle(block, copies):
    key_pos = lax.broadcasted_iota(jnp.int32, (block, copies * block), 0)
    query_pos = lax.broadcasted_iota(jnp.int32, (block, copies * block), 1)
    return key_pos <= lax.rem(query_pos, block)


def step_between(home, row, count):
    return home ^ row if count & (count - 1) == 0 else lax.rem(home - row + count, count)


def weights_kernel(qt_ref, s0_ref, own_ref, far_ref, near_ref, own_ids_ref, far_ids_ref, p_ref):
    block = s0_ref.shape[1]
    column = lax.axis_index("ctx")

    def seg_of(ref, core):
        cols = slice(core * block, (core + 1) * block)
        return ref[block : block + SEG_ROWS, cols].astype(F32)[0:1]

    first_core = lax.rem(column, 2) == 0
    seg_own = jnp.where(first_core, seg_of(own_ids_ref, 0), seg_of(own_ids_ref, 1))
    seg_near = jnp.where(first_core, seg_of(far_ids_ref, 1), seg_of(own_ids_ref, 0))
    seg_far = jnp.where(first_core, seg_of(far_ids_ref, 0), seg_of(far_ids_ref, 1))
    first = seg_own[:, 0:1]
    reach = jnp.where(column >= 1, jnp.sum((seg_near == first).astype(F32), axis=1, keepdims=True), 0.0)
    reach = reach + jnp.where(
        column >= 2, jnp.sum((seg_far == first).astype(F32), axis=1, keepdims=True), 0.0
    )
    key_pos = lax.broadcasted_iota(jnp.int32, (block, block), 0).astype(F32)
    tri = triangle(block, 1)
    seg_rows = jnp.broadcast_to(seg_own, (block, block))
    joined = seg_rows == first
    own_ok = seg_rows == seg_rows.T
    far_ok = (key_pos >= 2 * block - reach) & joined
    near_ok = (key_pos >= block - reach) & joined
    bias_x = jnp.where((tri & own_ok) | (~tri & far_ok), 0.0, NEG)
    bias_n = jnp.where(near_ok, 0.0, NEG)
    bias_x = jnp.concatenate([bias_x] * GROUP, axis=1)
    bias_n = jnp.concatenate([bias_n] * GROUP, axis=1)
    tri_g = triangle(block, GROUP)
    scaling = math.log2(math.e) / math.sqrt(HEAD_DIM)
    for g in range(qt_ref.shape[0]):
        keys = head_blocks(g, block, own_ref, far_ref, near_ref)
        scores = dot(jnp.concatenate(keys[1:], axis=0), qt_ref[g], NN)
        s_x = jnp.where(tri_g, s0_ref[g], scores[block:]) * scaling + bias_x
        s_n = scores[0:block] * scaling + bias_n
        highest = jnp.max(jnp.maximum(s_x, s_n), axis=0, keepdims=True)
        e_x = jnp.exp2(s_x - highest)
        e_n = jnp.exp2(s_n - highest)
        inverse = 1.0 / jnp.sum(e_x + e_n, axis=0, keepdims=True)
        p_ref[g, 0:block] = (e_x * inverse).astype(BF16)
        p_ref[g, block : 2 * block] = (e_n * inverse).astype(BF16)


def attend_kernel(n_dp, home_hbm, p_ref, own_ref, far_ref, near_ref, *rest):
    sends, (held, counts, filled, home_ref, sem) = rest[:n_dp], rest[n_dp:]
    fetch = pltpu.make_async_copy(home_hbm, home_ref, sem)
    fetch.start()
    block = near_ref.shape[0]
    row = lax.axis_index("dp")
    pieces = home_ref.shape[1]
    piece_len = block // pieces
    capacity = sends[0].shape[0]
    held[pieces] = jnp.zeros(held.shape[1:], held.dtype)
    lower = lower_mask(block)
    for g in range(p_ref.shape[0]):
        values = head_blocks(g, block, own_ref, far_ref, near_ref)
        w_0, w_2 = split(lower, p_ref[g, 0:block])
        weights = jnp.concatenate([w_0, p_ref[g, block : 2 * block], w_2], axis=0)
        attended = dot(jnp.concatenate(values, axis=0), weights, TN).astype(BF16)
        for h in range(GROUP):
            cols = slice((g * GROUP + h) * HEAD_DIM, (g * GROUP + h + 1) * HEAD_DIM)
            tile = attended[:, h * block : (h + 1) * block].T
            held[0:pieces, :, cols] = tile.reshape(pieces, piece_len, HEAD_DIM)
    fetch.wait()
    for d in range(n_dp):
        counts[d] = 0
        for slot in range(capacity):
            filled[d * capacity + slot] = pieces
    for m in range(pieces):
        step = step_between(home_ref[0, m], row, n_dp)
        slot = counts[step]
        counts[step] = slot + 1
        filled[step * capacity + slot] = m
    for d in range(n_dp - 1, -1, -1):
        for slot in range(capacity):
            sends[d][slot] = held[filled[d * capacity + slot]]


def split(lower, packed):
    own = packed * lower
    return own, packed - own


def lower_mask(block):
    return jnp.where(triangle(block, GROUP), 1.0, 0.0).astype(BF16)


def ahead_kernel(
    home_hbm, q_hbm, do_hbm, k_hbm, v_ref,
    plan_ref, qt_ref, gt_ref, s0_ref, gw0_ref, q_ref, do_ref, key_ref, sems,
):
    pairs = ((q_hbm, q_ref), (k_hbm, key_ref), (do_hbm, do_ref), (home_hbm, plan_ref))
    copies = [pltpu.make_async_copy(*pair, sems.at[i]) for i, pair in enumerate(pairs)]
    for copy in copies:
        copy.start()
    block = q_ref.shape[0]
    for source, own_ref, turned, product, waits in (
        (q_ref, key_ref, qt_ref, s0_ref, copies[:2]),
        (do_ref, v_ref, gt_ref, gw0_ref, copies[2:]),
    ):
        for copy in waits:
            copy.wait()
        for g in range(qt_ref.shape[0]):
            turned[g] = stacked(source, g).T
            product[g] = dot(own_ref[0:block, g * HEAD_DIM : (g + 1) * HEAD_DIM], turned[g], NN)


def sent_kernel(q_ref, do_ref, gt_ref, gw0_ref, own_ref, far_ref, near_ref, p_ref, gs_ref, d2_ref, dk1_ref, dv1_ref):
    block = q_ref.shape[0]
    tri_g, lower = triangle(block, GROUP), lower_mask(block)
    scaling = 1.0 / math.sqrt(HEAD_DIM)
    for g in range(own_ref.shape[1] // HEAD_DIM):
        values = head_blocks(g, block, own_ref, far_ref, near_ref)
        queries, grads = stacked(q_ref, g), stacked(do_ref, g)
        w_xb = p_ref[g, 0:block]
        w_x = w_xb.astype(F32)
        w_n = p_ref[g, block : 2 * block]
        w_nf = w_n.astype(F32)
        score_terms = dot(jnp.concatenate(values[1:], axis=0), gt_ref[g], NN)
        gw_x = jnp.where(tri_g, gw0_ref[g], score_terms[block:])
        gw_n = score_terms[0:block]
        delta = jnp.sum(w_x * gw_x + w_nf * gw_n, axis=0, keepdims=True)
        gs_x = (w_x * (gw_x - delta) * scaling).astype(BF16)
        gs_n = (w_nf * (gw_n - delta) * scaling).astype(BF16)
        gs_ref[g, 0:block] = gs_x
        gs_ref[g, block : 2 * block] = gs_n
        _, gs_2 = split(lower, gs_x)
        _, w_2 = split(lower, w_xb)
        cols = slice(g * HEAD_DIM, (g + 1) * HEAD_DIM)
        dk = dot(jnp.concatenate([gs_n, gs_2], axis=0), queries, NN).astype(d2_ref.dtype)
        dv = dot(jnp.concatenate([w_n, w_2], axis=0), grads, NN).astype(d2_ref.dtype)
        dk1_ref[:, cols] = dk[0:block]
        dv1_ref[:, cols] = dv[0:block]
        d2_ref[0:block, cols] = dk[block:]
        d2_ref[block : 2 * block, cols] = dv[block:]


def kept_kernel(q_ref, do_ref, own_ref, far_ref, near_ref, p_ref, gs_ref, dq_ref, d0_ref, mark_ref):
    mark_ref[...] = jnp.zeros_like(mark_ref)
    block = q_ref.shape[0]
    lower = lower_mask(block)
    for g in range(own_ref.shape[1] // HEAD_DIM):
        keys = head_blocks(g, block, own_ref, far_ref, near_ref)
        queries, grads = stacked(q_ref, g), stacked(do_ref, g)
        gs_0, gs_2 = split(lower, gs_ref[g, 0:block])
        w_0, _ = split(lower, p_ref[g, 0:block])
        gs_n = gs_ref[g, block : 2 * block]
        cols = slice(g * HEAD_DIM, (g + 1) * HEAD_DIM)
        d0_ref[0:block, cols] = dot(gs_0, queries, NN)
        d0_ref[block : 2 * block, cols] = dot(w_0, grads, NN)
        dq = dot(jnp.concatenate([gs_0, gs_n, gs_2], axis=0), jnp.concatenate(keys, axis=0), TN)
        for h in range(GROUP):
            heads = slice((g * GROUP + h) * HEAD_DIM, (g * GROUP + h + 1) * HEAD_DIM)
            dq_ref[:, heads] = dq[h * block : (h + 1) * block].astype(dq_ref.dtype)


def bundle_kernel(seg_hbm, other_ref, v_hbm, own_ref, seg_ref, sems):
    block = v_hbm.shape[0]
    copies = [
        pltpu.make_async_copy(seg_hbm, seg_ref, sems.at[0]),
        pltpu.make_async_copy(v_hbm, own_ref.at[0:block], sems.at[1]),
    ]
    for copy in copies:
        copy.start()
    tail = slice(block, block + SEG_ROWS)
    own_ref[tail, 2 * block :] = jnp.zeros((SEG_ROWS, own_ref.shape[1] - 2 * block), BF16)
    first_core = lax.rem(lax.axis_index("ctx"), 2) == 0
    copies[0].wait()
    own_ids, other_ids = seg_ref[...].astype(F32), other_ref[...].astype(F32)
    ids = (jnp.where(first_core, own_ids, other_ids), jnp.where(first_core, other_ids, own_ids))
    for core in range(2):
        cols = slice(core * block, (core + 1) * block)
        own_ref[tail, cols] = jnp.broadcast_to(ids[core], (SEG_ROWS, block)).astype(BF16)
    copies[1].wait()


def pick_kernel(colours, own_ref, *rest):
    moved_refs, (_, out_ref, crossing_ref) = rest[:colours], rest[colours:]
    chip, core = lax.axis_index("ctx") // 2, lax.rem(lax.axis_index("ctx"), 2)
    colour = lax.rem(chip + colours - 1, colours)
    picked = moved_refs[0][...]
    for i in range(1, colours):
        picked = jnp.where(colour == colours - 1 - i, moved_refs[i][...], picked)
    out_ref[...] = picked
    block = min(own_ref.shape[0], crossing_ref.shape[0])
    crossing_ref[0:block] = jnp.where(core == 0, own_ref[0:block], picked[0:block])
    if crossing_ref.shape[0] > block:
        crossing_ref[block:] = jnp.zeros((crossing_ref.shape[0] - block, own_ref.shape[1]), BF16)


def merge_kernel(d2_ref, dk1_ref, dv1_ref, out_ref):
    block = dk1_ref.shape[0]
    odd = lax.rem(lax.axis_index("ctx"), 2) == 1
    for part, d1_ref in enumerate((dk1_ref, dv1_ref)):
        rows = slice(part * block, (part + 1) * block)
        other = jnp.where(odd, d1_ref[...].astype(F32), 0.0)
        out_ref[rows] = (d2_ref[rows].astype(F32) + other).astype(out_ref.dtype)


def source_row(row, step, count):
    return row ^ step if count & (count - 1) == 0 else lax.rem(row - step + count, count)


def early_kernel(n_dp, kept_ref, far_ref, own_ref, out_ref, sems):
    row = lax.axis_index("dp")
    copies = [
        pltpu.make_async_copy(own_ref, out_ref.at[0, 0, row], sems.at[0]),
        pltpu.make_async_copy(
            far_ref, out_ref.at[0, 0, source_row(row, n_dp - 1, n_dp)], sems.at[1]
        ),
    ]
    for copy in copies:
        copy.start()
    for copy in copies:
        copy.wait()


def finish_kernel(n_dp, n_ctx, *rest):
    pieces, rest = rest[: n_dp - 2], rest[n_dp - 2 :]
    uneven_ref, even_ref, dk1_ref, dv1_ref, d0_ref, _, out_ref, dk_ref, dv_ref, total_ref, sems = rest
    row, column = lax.axis_index("dp"), lax.axis_index("ctx")
    block = dk_ref.shape[0]
    copies = []
    for i in range(n_dp - 2):
        target = out_ref.at[0, 0, source_row(row, n_dp - 2 - i, n_dp)]
        copies.append(pltpu.make_async_copy(pieces[i], target, sems.at[i]))
        copies[-1].start()
    for part, (d1_ref, target) in enumerate(((dk1_ref, dk_ref), (dv1_ref, dv_ref))):
        rows = slice(part * block, (part + 1) * block)
        total = d0_ref[rows]
        total = total + jnp.where(lax.rem(column, 2) == 0, d1_ref[...].astype(F32), 0.0)
        d2 = jnp.where(lax.rem(column // 2, 2) == 0, even_ref[rows], uneven_ref[rows])
        total = total + jnp.where(column + 2 < n_ctx, d2.astype(F32), 0.0)
        total_ref[rows] = total.astype(total_ref.dtype)
        copies.append(pltpu.make_async_copy(total_ref.at[rows], target, sems.at[n_dp - 2 + part]))
        copies[-1].start()
    for copy in copies:
        copy.wait()


VMEM = pl.BlockSpec(memory_space=pltpu.VMEM)
HBM = pl.BlockSpec(memory_space=pl.ANY)


def params(kib=32 * 1024):
    return pltpu.CompilerParams(vmem_limit_bytes=kib * 1024)


def cost(flops, nbytes):
    return pl.CostEstimate(flops=flops, bytes_accessed=nbytes, transcendentals=0)


def pinned(*arrays):
    return [pltpu.with_memory_space_constraint(array, pltpu.HBM) for array in arrays]


def swap(value):
    count = lax.axis_size("ctx")
    return lax.ppermute(value, "ctx", [(i, i ^ 1) for i in range(count)])


def from_chip(value, colours):
    count = lax.axis_size("ctx")

    def pairs(colour):
        found = []
        for i in range(count):
            chip, core = i // 2, i % 2
            other = chip + 1 if chip % colours == colour else chip - 1 if (chip - 1) % colours == colour else -1
            found.append((i, 2 * other + core if 0 <= other < count // 2 else i ^ 1))
        return found

    return [lax.ppermute(value, "ctx", pairs(colour)) for colour in range(colours)]


def exchange(value, k):
    count = lax.axis_size("dp")
    if count & (count - 1) == 0:
        pairs = [(i, i ^ k) for i in range(count)]
    else:
        pairs = [(i, (i + k) % count) for i in range(count)]
    return lax.ppermute(value, "dp", pairs)


def on_device(query_rows, key_rows, value_rows, out_grad, segment_ids, home_rows):
    n_dp, n_ctx = lax.axis_size("dp"), lax.axis_size("ctx")
    query, grad = query_rows[0], out_grad[0]
    block, width = query.shape
    kv_width = key_rows.shape[2]
    heads = kv_width // HEAD_DIM
    pieces = home_rows.shape[1]
    capacity = max(2, 2 * pieces // n_dp)
    piece_len = block // pieces
    column = lax.axis_index("ctx")
    keys = key_rows[0]
    moved_keys = from_chip(keys, 3)
    values = pl.pallas_call(
        bundle_kernel,
        out_shape=jax.ShapeDtypeStruct((block + SEG_ROWS, kv_width), BF16),
        in_specs=[HBM, VMEM, HBM],
        out_specs=VMEM,
        scratch_shapes=[pltpu.VMEM((1, block), jnp.int32), pltpu.SemaphoreType.DMA((2,))],
        compiler_params=params(),
        cost_estimate=cost(0, 0),
        name="bundle",
    )(*pinned(segment_ids), swap(segment_ids), *pinned(value_rows[0]))
    moved_values = from_chip(values, 2)

    turned = jax.ShapeDtypeStruct((heads, HEAD_DIM, GROUP * block), BF16)
    product = jax.ShapeDtypeStruct((heads, block, GROUP * block), F32)
    plan, turned_query, turned_grad, own_scores, own_terms, query, grad, own_keys = pl.pallas_call(
        ahead_kernel,
        out_shape=[
            jax.ShapeDtypeStruct(home_rows.shape, jnp.int32), turned, turned, product, product,
            jax.ShapeDtypeStruct(query.shape, BF16), jax.ShapeDtypeStruct(grad.shape, BF16),
            jax.ShapeDtypeStruct(keys.shape, BF16),
        ],
        in_specs=[HBM] * 4 + [VMEM],
        out_specs=[VMEM] * 8,
        scratch_shapes=[pltpu.SemaphoreType.DMA((4,))],
        compiler_params=params(),
        cost_estimate=cost(0, 0),
        name="ahead",
    )(*pinned(home_rows, query, grad, keys), values)
    far_keys, crossing = pl.pallas_call(
        functools.partial(pick_kernel, len(moved_keys)),
        out_shape=[
            jax.ShapeDtypeStruct(keys.shape, BF16), jax.ShapeDtypeStruct(values.shape, BF16)
        ],
        in_specs=[VMEM] * (1 + len(moved_keys)) + [HBM],
        out_specs=[VMEM] * 2,
        compiler_params=params(),
        cost_estimate=cost(0, 0),
        name="pick_keys",
    )(own_keys, *moved_keys[::-1], plan)
    near_keys = swap(crossing)
    far_values, crossing = pl.pallas_call(
        functools.partial(pick_kernel, len(moved_values)),
        out_shape=[
            jax.ShapeDtypeStruct(values.shape, BF16), jax.ShapeDtypeStruct(keys.shape, BF16)
        ],
        in_specs=[VMEM] * (1 + len(moved_values)) + [HBM],
        out_specs=[VMEM] * 2,
        compiler_params=params(),
        cost_estimate=cost(0, 0),
        name="pick_values",
    )(values, *moved_values[::-1], plan)
    near_values = swap(crossing)
    weights = pl.pallas_call(
        weights_kernel,
        out_shape=jax.ShapeDtypeStruct((heads, 2 * block, GROUP * block), BF16),
        in_specs=[VMEM] * 7,
        out_specs=VMEM,
        compiler_params=params(),
        cost_estimate=cost(0, 0),
        name="weights",
    )(turned_query, own_scores, own_keys, far_keys, near_keys, values, far_values)
    sends = pl.pallas_call(
        functools.partial(attend_kernel, n_dp),
        out_shape=[jax.ShapeDtypeStruct((capacity, piece_len, width), BF16)] * n_dp,
        in_specs=[HBM] + [VMEM] * 4,
        out_specs=[VMEM] * n_dp,
        scratch_shapes=[
            pltpu.VMEM((pieces + 1, piece_len, width), BF16),
            pltpu.SMEM((n_dp,), jnp.int32),
            pltpu.SMEM((n_dp * capacity,), jnp.int32),
            pltpu.SMEM((1, pieces), jnp.int32),
            pltpu.SemaphoreType.DMA,
        ],
        compiler_params=params(),
        cost_estimate=cost(0, 0),
        name="attend",
    )(plan, weights, values, far_values, near_values)
    arrived = [exchange(sends[k], k) for k in range(n_dp - 1, 0, -1)] + [sends[0]]
    terms = jax.ShapeDtypeStruct((2 * block, kv_width), BF16)
    half = jax.ShapeDtypeStruct((block, kv_width), BF16)
    mark = jax.ShapeDtypeStruct((8, HEAD_DIM), F32)
    score_grads, d2, dk1, dv1 = pl.pallas_call(
        sent_kernel,
        out_shape=[jax.ShapeDtypeStruct(weights.shape, BF16), terms, half, half],
        in_specs=[VMEM] * 8,
        out_specs=[VMEM] * 4,
        compiler_params=params(),
        cost_estimate=cost(0, 0),
        name="sent_terms",
    )(query, grad, turned_grad, own_terms, values, far_values, near_values, weights)
    dq, d0, after_kept = pl.pallas_call(
        kept_kernel,
        out_shape=[
            jax.ShapeDtypeStruct((block, width), BF16),
            jax.ShapeDtypeStruct((2 * block, kv_width), F32),
            mark,
        ],
        in_specs=[VMEM] * 7,
        out_specs=[VMEM] * 3,
        compiler_params=params(),
        cost_estimate=cost(1073741824, 0),
        name="kept_terms",
    )(query, grad, own_keys, far_keys, near_keys, weights, score_grads)
    dk1_in, dv1_in = swap(dk1), swap(dv1)
    d2_sum = pl.pallas_call(
        merge_kernel,
        out_shape=terms,
        in_specs=[VMEM] * 3,
        out_specs=VMEM,
        compiler_params=params(),
        cost_estimate=cost(0, 0),
        name="merge",
    )(d2, dk1_in, dv1_in)
    d2_even, d2_uneven = from_chip(d2_sum, 2)
    routed_shape = jax.ShapeDtypeStruct((1, 1, n_dp, capacity, piece_len, width), BF16)
    routed = pl.pallas_call(
        functools.partial(early_kernel, n_dp),
        out_shape=routed_shape,
        in_specs=[HBM] * 3,
        out_specs=HBM,
        scratch_shapes=[pltpu.SemaphoreType.DMA((2,))],
        compiler_params=params(),
        cost_estimate=cost(2147483648, 0),
        name="place_early",
    )(after_kept, arrived[0], arrived[-1])
    routed, dk, dv = pl.pallas_call(
        functools.partial(finish_kernel, n_dp, n_ctx),
        out_shape=[routed_shape] + [jax.ShapeDtypeStruct((block, kv_width), BF16)] * 2,
        in_specs=[HBM] * (n_dp - 2) + [VMEM] * 5 + [HBM],
        out_specs=[HBM] * 3,
        input_output_aliases={n_dp + 3: 0},
        scratch_shapes=[
            pltpu.VMEM((2 * block, kv_width), BF16),
            pltpu.SemaphoreType.DMA((n_dp,)),
        ],
        compiler_params=params(),
        cost_estimate=cost(0, 1 << 20),
        name="finish",
    )(*arrived[1:-1], d2_uneven, d2_even, dk1_in, dv1_in, d0, *pinned(routed))
    return routed, dq[None], dk[None], dv[None]


def solution(mesh):
    rows = P("dp", "ctx", None)
    return jax.shard_map(
        on_device,
        mesh=mesh,
        in_specs=(rows, rows, rows, rows, P("dp", "ctx"), P("dp", "ctx")),
        out_specs=(P("dp", "ctx", None, None, None, None), rows, rows, rows),
        check_vma=False,
    )
```

```python
import functools
import math

import jax
import jax.numpy as jnp
from jax import lax
from jax.experimental import pallas as pl
from jax.experimental.pallas import tpu as pltpu
from jax.sharding import PartitionSpec as P

HEAD_DIM = 128
GROUP = 4
SEG_ROWS = 16
F32 = jnp.float32
BF16 = jnp.bfloat16
NEG = -1e30

NT = (((1,), (1,)), ((), ()))
NN = (((1,), (0,)), ((), ()))
TN = (((0,), (0,)), ((), ()))


def dot(a, b, dims):
    return lax.dot_general(a, b, dims, preferred_element_type=F32)


def stacked(ref, g):
    heads = [
        ref[:, (g * GROUP + h) * HEAD_DIM : (g * GROUP + h + 1) * HEAD_DIM] for h in range(GROUP)
    ]
    return jnp.concatenate(heads, axis=0)


def head_blocks(g, block, own_ref, far_ref, near_ref):
    cols = slice(g * HEAD_DIM, (g + 1) * HEAD_DIM)
    return [ref[0:block, cols] for ref in (own_ref, near_ref, far_ref)]


def triangle(block, copies):
    key_pos = lax.broadcasted_iota(jnp.int32, (block, copies * block), 0)
    query_pos = lax.broadcasted_iota(jnp.int32, (block, copies * block), 1)
    return key_pos <= lax.rem(query_pos, block)


def step_between(home, row, count):
    return home ^ row if count & (count - 1) == 0 else lax.rem(home - row + count, count)


def weights_kernel(
    qt_ref, s0_ref, own_ref, far_ref, near_ref, own_ids_ref, far_ids_ref, bias_ref, joined_ref, p_ref
):
    block = s0_ref.shape[1]
    column = lax.axis_index("ctx")

    first_core = lax.rem(column, 2) == 0
    first = own_ids(own_ids_ref, block)[:, 0:1]
    seg_near = jnp.where(first_core, ids_of(far_ids_ref, block, 1), ids_of(own_ids_ref, block, 0))
    seg_far = jnp.where(first_core, ids_of(far_ids_ref, block, 0), ids_of(far_ids_ref, block, 1))
    seen = jnp.where((seg_near == first) & (column >= 1), 1.0, 0.0)
    seen = seen + jnp.where((seg_far == first) & (column >= 2), 1.0, 0.0)
    reach = jnp.sum(seen, axis=1, keepdims=True)
    key_pos = lax.broadcasted_iota(jnp.int32, (block, block), 0).astype(F32)
    joined = joined_ref[...]
    far_bias = jnp.where(key_pos >= 2 * block - reach, joined, NEG)
    bias_n = jnp.where(key_pos >= block - reach, joined, NEG)
    bias_x = jnp.where(triangle(block, 1), bias_ref[...], far_bias)
    bias_x = jnp.concatenate([bias_x] * GROUP, axis=1)
    bias_n = jnp.concatenate([bias_n] * GROUP, axis=1)
    tri_g = triangle(block, GROUP)
    scaling = math.log2(math.e) / math.sqrt(HEAD_DIM)
    def products(g):
        keys = head_blocks(g, block, own_ref, far_ref, near_ref)
        return dot(jnp.concatenate(keys[1:], axis=0), qt_ref[g], NN)

    heads = qt_ref.shape[0]
    upcoming = products(0)
    for g in range(heads):
        scores, upcoming = upcoming, products(g + 1) if g + 1 < heads else None
        s_x = jnp.where(tri_g, s0_ref[g], scores[block:]) * scaling + bias_x
        s_n = scores[0:block] * scaling + bias_n
        highest = jnp.max(jnp.maximum(s_x, s_n), axis=0, keepdims=True)
        e_x = jnp.exp2(s_x - highest)
        e_n = jnp.exp2(s_n - highest)
        inverse = 1.0 / jnp.sum(e_x + e_n, axis=0, keepdims=True)
        p_ref[g, 0:block] = (e_x * inverse).astype(BF16)
        p_ref[g, block : 2 * block] = (e_n * inverse).astype(BF16)


def attend_kernel(n_dp, home_hbm, p_ref, own_ref, far_ref, near_ref, *rest):
    sends, (held, counts, filled, home_ref, sem) = rest[:n_dp], rest[n_dp:]
    fetch = pltpu.make_async_copy(home_hbm, home_ref, sem)
    fetch.start()
    block = near_ref.shape[0]
    row = lax.axis_index("dp")
    pieces = home_ref.shape[1]
    piece_len = block // pieces
    capacity = sends[0].shape[0]
    held[pieces] = jnp.zeros(held.shape[1:], held.dtype)
    lower = lower_mask(block)
    for g in range(p_ref.shape[0]):
        values = head_blocks(g, block, own_ref, far_ref, near_ref)
        w_0, w_2 = split(lower, p_ref[g, 0:block])
        weights = jnp.concatenate([w_0, p_ref[g, block : 2 * block], w_2], axis=0)
        attended = dot(jnp.concatenate(values, axis=0), weights, TN).astype(BF16)
        for h in range(GROUP):
            cols = slice((g * GROUP + h) * HEAD_DIM, (g * GROUP + h + 1) * HEAD_DIM)
            tile = attended[:, h * block : (h + 1) * block].T
            held[0:pieces, :, cols] = tile.reshape(pieces, piece_len, HEAD_DIM)
    fetch.wait()
    for d in range(n_dp):
        counts[d] = 0
        for slot in range(capacity):
            filled[d * capacity + slot] = pieces
    for m in range(pieces):
        step = step_between(home_ref[0, m], row, n_dp)
        slot = counts[step]
        counts[step] = slot + 1
        filled[step * capacity + slot] = m
    for d in range(n_dp - 1, -1, -1):
        for slot in range(capacity):
            sends[d][slot] = held[filled[d * capacity + slot]]


def split(lower, packed):
    own = packed * lower
    return own, packed - own


def lower_mask(block):
    return jnp.where(triangle(block, GROUP), 1.0, 0.0).astype(BF16)


def ids_of(ref, block, core):
    cols = slice(core * block, (core + 1) * block)
    return ref[block : block + SEG_ROWS, cols].astype(F32)[0:1]


def own_ids(ref, block):
    first_core = lax.rem(lax.axis_index("ctx"), 2) == 0
    return jnp.where(first_core, ids_of(ref, block, 0), ids_of(ref, block, 1))


def ahead_kernel(
    home_hbm, q_hbm, do_hbm, k_hbm, v_ref,
    plan_ref, qt_ref, gt_ref, s0_ref, gw0_ref, q_ref, do_ref, key_ref, bias_ref, joined_ref, sems,
):
    pairs = ((q_hbm, q_ref), (k_hbm, key_ref), (do_hbm, do_ref), (home_hbm, plan_ref))
    copies = [pltpu.make_async_copy(*pair, sems.at[i]) for i, pair in enumerate(pairs)]
    for copy in copies:
        copy.start()
    block = q_ref.shape[0]
    seg_own = own_ids(v_ref, block)
    seg_rows = jnp.broadcast_to(seg_own, (block, block))
    own_ok = triangle(block, 1) & (seg_rows == seg_rows.T)
    bias_ref[...] = jnp.where(own_ok, 0.0, NEG)
    joined_ref[...] = jnp.where(seg_rows == seg_own[:, 0:1], 0.0, NEG)
    for source, own_ref, turned, product, waits in (
        (q_ref, key_ref, qt_ref, s0_ref, copies[:2]),
        (do_ref, v_ref, gt_ref, gw0_ref, copies[2:]),
    ):
        for copy in waits:
            copy.wait()
        for g in range(qt_ref.shape[0]):
            turned[g] = stacked(source, g).T
            product[g] = dot(own_ref[0:block, g * HEAD_DIM : (g + 1) * HEAD_DIM], turned[g], NN)


def sent_kernel(q_ref, do_ref, gt_ref, gw0_ref, own_ref, far_ref, near_ref, p_ref, gs_ref, d2_ref, dk1_ref, dv1_ref):
    block = q_ref.shape[0]
    tri_g, lower = triangle(block, GROUP), lower_mask(block)
    scaling = 1.0 / math.sqrt(HEAD_DIM)
    def products(g):
        values = head_blocks(g, block, own_ref, far_ref, near_ref)
        return dot(jnp.concatenate(values[1:], axis=0), gt_ref[g], NN)

    heads = gt_ref.shape[0]
    upcoming = products(0)
    for g in range(heads):
        score_terms, upcoming = upcoming, products(g + 1) if g + 1 < heads else None
        queries, grads = stacked(q_ref, g), stacked(do_ref, g)
        w_xb = p_ref[g, 0:block]
        w_x = w_xb.astype(F32)
        w_n = p_ref[g, block : 2 * block]
        w_nf = w_n.astype(F32)
        gw_x = jnp.where(tri_g, gw0_ref[g], score_terms[block:])
        gw_n = score_terms[0:block]
        delta = jnp.sum(w_x * gw_x + w_nf * gw_n, axis=0, keepdims=True)
        gs_x = (w_x * (gw_x - delta)).astype(BF16)
        gs_n = (w_nf * (gw_n - delta)).astype(BF16)
        gs_ref[g, 0:block] = gs_x
        gs_ref[g, block : 2 * block] = gs_n
        _, gs_2 = split(lower, gs_x)
        _, w_2 = split(lower, w_xb)
        cols = slice(g * HEAD_DIM, (g + 1) * HEAD_DIM)
        dk = (dot(jnp.concatenate([gs_n, gs_2], axis=0), queries, NN) * scaling).astype(d2_ref.dtype)
        dv = dot(jnp.concatenate([w_n, w_2], axis=0), grads, NN).astype(d2_ref.dtype)
        dk1_ref[:, cols] = dk[0:block]
        dv1_ref[:, cols] = dv[0:block]
        d2_ref[0:block, cols] = dk[block:]
        d2_ref[block : 2 * block, cols] = dv[block:]


def kept_kernel(q_ref, do_ref, own_ref, far_ref, near_ref, p_ref, gs_ref, dq_ref, d0_ref, mark_ref):
    mark_ref[...] = jnp.zeros_like(mark_ref)
    block = q_ref.shape[0]
    lower = lower_mask(block)
    scaling = 1.0 / math.sqrt(HEAD_DIM)
    for g in range(own_ref.shape[1] // HEAD_DIM):
        keys = head_blocks(g, block, own_ref, far_ref, near_ref)
        queries, grads = stacked(q_ref, g), stacked(do_ref, g)
        gs_0, gs_2 = split(lower, gs_ref[g, 0:block])
        w_0, _ = split(lower, p_ref[g, 0:block])
        gs_n = gs_ref[g, block : 2 * block]
        cols = slice(g * HEAD_DIM, (g + 1) * HEAD_DIM)
        d0_ref[0:block, cols] = dot(gs_0, queries, NN) * scaling
        d0_ref[block : 2 * block, cols] = dot(w_0, grads, NN)
        dq = dot(jnp.concatenate([gs_0, gs_n, gs_2], axis=0), jnp.concatenate(keys, axis=0), TN)
        for h in range(GROUP):
            heads = slice((g * GROUP + h) * HEAD_DIM, (g * GROUP + h + 1) * HEAD_DIM)
            dq_ref[:, heads] = (dq[h * block : (h + 1) * block] * scaling).astype(dq_ref.dtype)


def bundle_kernel(seg_hbm, other_ref, v_hbm, own_ref, seg_ref, sems):
    block = v_hbm.shape[0]
    copies = [
        pltpu.make_async_copy(seg_hbm, seg_ref, sems.at[0]),
        pltpu.make_async_copy(v_hbm, own_ref.at[0:block], sems.at[1]),
    ]
    for copy in copies:
        copy.start()
    tail = slice(block, block + SEG_ROWS)
    own_ref[tail, 2 * block :] = jnp.zeros((SEG_ROWS, own_ref.shape[1] - 2 * block), BF16)
    first_core = lax.rem(lax.axis_index("ctx"), 2) == 0
    copies[0].wait()
    own_ids, other_ids = seg_ref[...].astype(F32), other_ref[...].astype(F32)
    ids = (jnp.where(first_core, own_ids, other_ids), jnp.where(first_core, other_ids, own_ids))
    for core in range(2):
        cols = slice(core * block, (core + 1) * block)
        own_ref[tail, cols] = jnp.broadcast_to(ids[core], (SEG_ROWS, block)).astype(BF16)
    copies[1].wait()


def pick_kernel(colours, own_ref, *rest):
    moved_refs, (_, out_ref, crossing_ref) = rest[:colours], rest[colours:]
    chip, core = lax.axis_index("ctx") // 2, lax.rem(lax.axis_index("ctx"), 2)
    colour = lax.rem(chip + colours - 1, colours)
    picked = moved_refs[0][...]
    for i in range(1, colours):
        picked = jnp.where(colour == colours - 1 - i, moved_refs[i][...], picked)
    out_ref[...] = picked
    block = min(own_ref.shape[0], crossing_ref.shape[0])
    crossing_ref[0:block] = jnp.where(core == 0, own_ref[0:block], picked[0:block])
    if crossing_ref.shape[0] > block:
        crossing_ref[block:] = jnp.zeros((crossing_ref.shape[0] - block, own_ref.shape[1]), BF16)


def merge_kernel(d2_ref, dk1_ref, dv1_ref, out_ref):
    block = dk1_ref.shape[0]
    odd = lax.rem(lax.axis_index("ctx"), 2) == 1
    for part, d1_ref in enumerate((dk1_ref, dv1_ref)):
        rows = slice(part * block, (part + 1) * block)
        other = jnp.where(odd, d1_ref[...].astype(F32), 0.0)
        out_ref[rows] = (d2_ref[rows].astype(F32) + other).astype(out_ref.dtype)


def source_row(row, step, count):
    return row ^ step if count & (count - 1) == 0 else lax.rem(row - step + count, count)


def early_kernel(n_dp, kept_ref, far_ref, own_ref, out_ref, sems):
    row = lax.axis_index("dp")
    copies = [
        pltpu.make_async_copy(own_ref, out_ref.at[0, 0, row], sems.at[0]),
        pltpu.make_async_copy(
            far_ref, out_ref.at[0, 0, source_row(row, n_dp - 1, n_dp)], sems.at[1]
        ),
    ]
    for copy in copies:
        copy.start()
    for copy in copies:
        copy.wait()


def finish_kernel(n_dp, n_ctx, *rest):
    pieces, rest = rest[: n_dp - 2], rest[n_dp - 2 :]
    uneven_ref, even_ref, dk1_ref, dv1_ref, d0_ref, _, out_ref, dk_ref, dv_ref, total_ref, sems = rest
    row, column = lax.axis_index("dp"), lax.axis_index("ctx")
    block = dk_ref.shape[0]
    copies = []
    for i in range(n_dp - 2):
        target = out_ref.at[0, 0, source_row(row, n_dp - 2 - i, n_dp)]
        copies.append(pltpu.make_async_copy(pieces[i], target, sems.at[i]))
        copies[-1].start()
    for part, (d1_ref, target) in enumerate(((dk1_ref, dk_ref), (dv1_ref, dv_ref))):
        rows = slice(part * block, (part + 1) * block)
        total = d0_ref[rows]
        total = total + jnp.where(lax.rem(column, 2) == 0, d1_ref[...].astype(F32), 0.0)
        d2 = jnp.where(lax.rem(column // 2, 2) == 0, even_ref[rows], uneven_ref[rows])
        total = total + jnp.where(column + 2 < n_ctx, d2.astype(F32), 0.0)
        total_ref[rows] = total.astype(total_ref.dtype)
        copies.append(pltpu.make_async_copy(total_ref.at[rows], target, sems.at[n_dp - 2 + part]))
        copies[-1].start()
    for copy in copies:
        copy.wait()


VMEM = pl.BlockSpec(memory_space=pltpu.VMEM)
HBM = pl.BlockSpec(memory_space=pl.ANY)


def params(kib=32 * 1024):
    return pltpu.CompilerParams(vmem_limit_bytes=kib * 1024)


def cost(flops, nbytes):
    return pl.CostEstimate(flops=flops, bytes_accessed=nbytes, transcendentals=0)


def pinned(*arrays):
    return [pltpu.with_memory_space_constraint(array, pltpu.HBM) for array in arrays]


def swap(value):
    count = lax.axis_size("ctx")
    return lax.ppermute(value, "ctx", [(i, i ^ 1) for i in range(count)])


def from_chip(value, colours):
    count = lax.axis_size("ctx")

    def pairs(colour):
        found = []
        for i in range(count):
            chip, core = i // 2, i % 2
            other = chip + 1 if chip % colours == colour else chip - 1 if (chip - 1) % colours == colour else -1
            found.append((i, 2 * other + core if 0 <= other < count // 2 else i ^ 1))
        return found

    return [lax.ppermute(value, "ctx", pairs(colour)) for colour in range(colours)]


def exchange(value, k):
    count = lax.axis_size("dp")
    if count & (count - 1) == 0:
        pairs = [(i, i ^ k) for i in range(count)]
    else:
        pairs = [(i, (i + k) % count) for i in range(count)]
    return lax.ppermute(value, "dp", pairs)


def on_device(query_rows, key_rows, value_rows, out_grad, segment_ids, home_rows):
    n_dp, n_ctx = lax.axis_size("dp"), lax.axis_size("ctx")
    query, grad = query_rows[0], out_grad[0]
    block, width = query.shape
    kv_width = key_rows.shape[2]
    heads = kv_width // HEAD_DIM
    pieces = home_rows.shape[1]
    capacity = max(2, 2 * pieces // n_dp)
    piece_len = block // pieces
    column = lax.axis_index("ctx")
    keys = key_rows[0]
    moved_keys = from_chip(keys, 3)
    values = pl.pallas_call(
        bundle_kernel,
        out_shape=jax.ShapeDtypeStruct((block + SEG_ROWS, kv_width), BF16),
        in_specs=[HBM, VMEM, HBM],
        out_specs=VMEM,
        scratch_shapes=[pltpu.VMEM((1, block), jnp.int32), pltpu.SemaphoreType.DMA((2,))],
        compiler_params=params(),
        cost_estimate=cost(0, 0),
        name="bundle",
    )(*pinned(segment_ids), swap(segment_ids), *pinned(value_rows[0]))
    moved_values = from_chip(values, 2)

    turned = jax.ShapeDtypeStruct((heads, HEAD_DIM, GROUP * block), BF16)
    product = jax.ShapeDtypeStruct((heads, block, GROUP * block), F32)
    plan, turned_query, turned_grad, own_scores, own_terms, query, grad, own_keys, *masks = pl.pallas_call(
        ahead_kernel,
        out_shape=[
            jax.ShapeDtypeStruct(home_rows.shape, jnp.int32), turned, turned, product, product,
            jax.ShapeDtypeStruct(query.shape, BF16), jax.ShapeDtypeStruct(grad.shape, BF16),
            jax.ShapeDtypeStruct(keys.shape, BF16),
            jax.ShapeDtypeStruct((block, block), F32), jax.ShapeDtypeStruct((block, block), F32),
        ],
        in_specs=[HBM] * 4 + [VMEM],
        out_specs=[VMEM] * 10,
        scratch_shapes=[pltpu.SemaphoreType.DMA((4,))],
        compiler_params=params(),
        cost_estimate=cost(0, 0),
        name="ahead",
    )(*pinned(home_rows, query, grad, keys), values)
    far_keys, crossing = pl.pallas_call(
        functools.partial(pick_kernel, len(moved_keys)),
        out_shape=[
            jax.ShapeDtypeStruct(keys.shape, BF16), jax.ShapeDtypeStruct(values.shape, BF16)
        ],
        in_specs=[VMEM] * (1 + len(moved_keys)) + [HBM],
        out_specs=[VMEM] * 2,
        compiler_params=params(),
        cost_estimate=cost(0, 0),
        name="pick_keys",
    )(own_keys, *moved_keys[::-1], plan)
    near_keys = swap(crossing)
    far_values, crossing = pl.pallas_call(
        functools.partial(pick_kernel, len(moved_values)),
        out_shape=[
            jax.ShapeDtypeStruct(values.shape, BF16), jax.ShapeDtypeStruct(keys.shape, BF16)
        ],
        in_specs=[VMEM] * (1 + len(moved_values)) + [HBM],
        out_specs=[VMEM] * 2,
        compiler_params=params(),
        cost_estimate=cost(0, 0),
        name="pick_values",
    )(values, *moved_values[::-1], plan)
    near_values = swap(crossing)
    weights = pl.pallas_call(
        weights_kernel,
        out_shape=jax.ShapeDtypeStruct((heads, 2 * block, GROUP * block), BF16),
        in_specs=[VMEM] * 9,
        out_specs=VMEM,
        compiler_params=params(),
        cost_estimate=cost(0, 0),
        name="weights",
    )(turned_query, own_scores, own_keys, far_keys, near_keys, values, far_values, *masks)
    sends = pl.pallas_call(
        functools.partial(attend_kernel, n_dp),
        out_shape=[jax.ShapeDtypeStruct((capacity, piece_len, width), BF16)] * n_dp,
        in_specs=[HBM] + [VMEM] * 4,
        out_specs=[VMEM] * n_dp,
        scratch_shapes=[
            pltpu.VMEM((pieces + 1, piece_len, width), BF16),
            pltpu.SMEM((n_dp,), jnp.int32),
            pltpu.SMEM((n_dp * capacity,), jnp.int32),
            pltpu.SMEM((1, pieces), jnp.int32),
            pltpu.SemaphoreType.DMA,
        ],
        compiler_params=params(),
        cost_estimate=cost(0, 0),
        name="attend",
    )(plan, weights, values, far_values, near_values)
    arrived = [exchange(sends[k], k) for k in range(n_dp - 1, 0, -1)] + [sends[0]]
    terms = jax.ShapeDtypeStruct((2 * block, kv_width), BF16)
    half = jax.ShapeDtypeStruct((block, kv_width), BF16)
    mark = jax.ShapeDtypeStruct((8, HEAD_DIM), F32)
    score_grads, d2, dk1, dv1 = pl.pallas_call(
        sent_kernel,
        out_shape=[jax.ShapeDtypeStruct(weights.shape, BF16), terms, half, half],
        in_specs=[VMEM] * 8,
        out_specs=[VMEM] * 4,
        compiler_params=params(),
        cost_estimate=cost(0, 0),
        name="sent_terms",
    )(query, grad, turned_grad, own_terms, values, far_values, near_values, weights)
    dq, d0, after_kept = pl.pallas_call(
        kept_kernel,
        out_shape=[
            jax.ShapeDtypeStruct((block, width), BF16),
            jax.ShapeDtypeStruct((2 * block, kv_width), F32),
            mark,
        ],
        in_specs=[VMEM] * 7,
        out_specs=[VMEM] * 3,
        compiler_params=params(),
        cost_estimate=cost(1073741824, 0),
        name="kept_terms",
    )(query, grad, own_keys, far_keys, near_keys, weights, score_grads)
    dk1_in, dv1_in = swap(dk1), swap(dv1)
    d2_sum = pl.pallas_call(
        merge_kernel,
        out_shape=terms,
        in_specs=[VMEM] * 3,
        out_specs=VMEM,
        compiler_params=params(),
        cost_estimate=cost(0, 0),
        name="merge",
    )(d2, dk1_in, dv1_in)
    d2_even, d2_uneven = from_chip(d2_sum, 2)
    routed_shape = jax.ShapeDtypeStruct((1, 1, n_dp, capacity, piece_len, width), BF16)
    routed = pl.pallas_call(
        functools.partial(early_kernel, n_dp),
        out_shape=routed_shape,
        in_specs=[HBM] * 3,
        out_specs=HBM,
        scratch_shapes=[pltpu.SemaphoreType.DMA((2,))],
        compiler_params=params(),
        cost_estimate=cost(2147483648, 0),
        name="place_early",
    )(after_kept, arrived[0], arrived[-1])
    routed, dk, dv = pl.pallas_call(
        functools.partial(finish_kernel, n_dp, n_ctx),
        out_shape=[routed_shape] + [jax.ShapeDtypeStruct((block, kv_width), BF16)] * 2,
        in_specs=[HBM] * (n_dp - 2) + [VMEM] * 5 + [HBM],
        out_specs=[HBM] * 3,
        input_output_aliases={n_dp + 3: 0},
        scratch_shapes=[
            pltpu.VMEM((2 * block, kv_width), BF16),
            pltpu.SemaphoreType.DMA((n_dp,)),
        ],
        compiler_params=params(),
        cost_estimate=cost(0, 1 << 20),
        name="finish",
    )(*arrived[1:-1], d2_uneven, d2_even, dk1_in, dv1_in, d0, *pinned(routed))
    return routed, dq[None], dk[None], dv[None]


def solution(mesh):
    rows = P("dp", "ctx", None)
    return jax.shard_map(
        on_device,
        mesh=mesh,
        in_specs=(rows, rows, rows, rows, P("dp", "ctx"), P("dp", "ctx")),
        out_specs=(P("dp", "ctx", None, None, None, None), rows, rows, rows),
        check_vma=False,
    )
```

```python
import functools
import math

import jax
import jax.numpy as jnp
from jax import lax
from jax.experimental import pallas as pl
from jax.experimental.pallas import tpu as pltpu
from jax.sharding import PartitionSpec as P

HEAD_DIM = 128
GROUP = 4
SEG_ROWS = 16
F32 = jnp.float32
BF16 = jnp.bfloat16
NEG = -1e30

NT = (((1,), (1,)), ((), ()))
NN = (((1,), (0,)), ((), ()))
TN = (((0,), (0,)), ((), ()))


def dot(a, b, dims):
    return lax.dot_general(a, b, dims, preferred_element_type=F32)


def stacked(ref, g):
    heads = [
        ref[:, (g * GROUP + h) * HEAD_DIM : (g * GROUP + h + 1) * HEAD_DIM] for h in range(GROUP)
    ]
    return jnp.concatenate(heads, axis=0)


def head_blocks(g, block, own_ref, far_ref, near_ref):
    cols = slice(g * HEAD_DIM, (g + 1) * HEAD_DIM)
    return [ref[0:block, cols] for ref in (own_ref, near_ref, far_ref)]


def triangle(block, copies):
    key_pos = lax.broadcasted_iota(jnp.int32, (block, copies * block), 0)
    query_pos = lax.broadcasted_iota(jnp.int32, (block, copies * block), 1)
    return key_pos <= lax.rem(query_pos, block)


def step_between(home, row, count):
    return home ^ row if count & (count - 1) == 0 else lax.rem(home - row + count, count)


def weights_kernel(
    qt_ref, s0_ref, own_ref, far_ref, near_ref, own_ids_ref, far_ids_ref, bias_ref, joined_ref, p_ref
):
    block = s0_ref.shape[1]
    column = lax.axis_index("ctx")

    first_core = lax.rem(column, 2) == 0
    first = own_ids(own_ids_ref, block)[:, 0:1]
    seg_near = jnp.where(first_core, ids_of(far_ids_ref, block, 1), ids_of(own_ids_ref, block, 0))
    seg_far = jnp.where(first_core, ids_of(far_ids_ref, block, 0), ids_of(far_ids_ref, block, 1))
    seen = jnp.where((seg_near == first) & (column >= 1), 1.0, 0.0)
    seen = seen + jnp.where((seg_far == first) & (column >= 2), 1.0, 0.0)
    reach = jnp.sum(seen, axis=1, keepdims=True)
    key_pos = lax.broadcasted_iota(jnp.int32, (block, block), 0).astype(F32)
    joined = joined_ref[...]
    far_bias = jnp.where(key_pos >= 2 * block - reach, joined, NEG)
    bias_n = jnp.where(key_pos >= block - reach, joined, NEG)
    bias_x = jnp.where(triangle(block, 1), bias_ref[...], far_bias)
    tri = triangle(block, 1)
    scaling = math.log2(math.e) / math.sqrt(HEAD_DIM)
    def products(g):
        keys = head_blocks(g, block, own_ref, far_ref, near_ref)
        return dot(jnp.concatenate(keys[1:], axis=0), qt_ref[g], NN)

    heads = qt_ref.shape[0]
    upcoming = products(0)
    for g in range(heads):
        scores, upcoming = upcoming, products(g + 1) if g + 1 < heads else None
        for h in range(GROUP):
            cols = slice(h * block, (h + 1) * block)
            s_x = jnp.where(tri, s0_ref[g, :, cols], scores[block:, cols]) * scaling + bias_x
            s_n = scores[0:block, cols] * scaling + bias_n
            highest = jnp.max(jnp.maximum(s_x, s_n), axis=0, keepdims=True)
            e_x = jnp.exp2(s_x - highest)
            e_n = jnp.exp2(s_n - highest)
            inverse = 1.0 / jnp.sum(e_x + e_n, axis=0, keepdims=True)
            p_ref[g, 0:block, cols] = (e_x * inverse).astype(BF16)
            p_ref[g, block : 2 * block, cols] = (e_n * inverse).astype(BF16)


def attend_kernel(n_dp, home_hbm, p_ref, own_ref, far_ref, near_ref, *rest):
    sends, (held, counts, filled, home_ref, sem) = rest[:n_dp], rest[n_dp:]
    fetch = pltpu.make_async_copy(home_hbm, home_ref, sem)
    fetch.start()
    block = near_ref.shape[0]
    row = lax.axis_index("dp")
    pieces = home_ref.shape[1]
    piece_len = block // pieces
    capacity = sends[0].shape[0]
    held[pieces] = jnp.zeros(held.shape[1:], held.dtype)
    lower = lower_mask(block)
    for g in range(p_ref.shape[0]):
        values = head_blocks(g, block, own_ref, far_ref, near_ref)
        w_0, w_2 = split(lower, p_ref[g, 0:block])
        weights = jnp.concatenate([w_0, p_ref[g, block : 2 * block], w_2], axis=0)
        attended = dot(jnp.concatenate(values, axis=0), weights, TN).astype(BF16)
        for h in range(GROUP):
            cols = slice((g * GROUP + h) * HEAD_DIM, (g * GROUP + h + 1) * HEAD_DIM)
            tile = attended[:, h * block : (h + 1) * block].T
            held[0:pieces, :, cols] = tile.reshape(pieces, piece_len, HEAD_DIM)
    fetch.wait()
    for d in range(n_dp):
        counts[d] = 0
        for slot in range(capacity):
            filled[d * capacity + slot] = pieces
    for m in range(pieces):
        step = step_between(home_ref[0, m], row, n_dp)
        slot = counts[step]
        counts[step] = slot + 1
        filled[step * capacity + slot] = m
    for d in range(n_dp - 1, -1, -1):
        for slot in range(capacity):
            sends[d][slot] = held[filled[d * capacity + slot]]


def split(lower, packed):
    own = packed * lower
    return own, packed - own


def lower_mask(block):
    return jnp.where(triangle(block, GROUP), 1.0, 0.0).astype(BF16)


def ids_of(ref, block, core):
    cols = slice(core * block, (core + 1) * block)
    return ref[block : block + SEG_ROWS, cols].astype(F32)[0:1]


def own_ids(ref, block):
    first_core = lax.rem(lax.axis_index("ctx"), 2) == 0
    return jnp.where(first_core, ids_of(ref, block, 0), ids_of(ref, block, 1))


def ahead_kernel(
    home_hbm, q_hbm, do_hbm, k_hbm, v_ref,
    plan_ref, qt_ref, gt_ref, s0_ref, gw0_ref, q_ref, do_ref, key_ref, bias_ref, joined_ref, sems,
):
    pairs = ((q_hbm, q_ref), (k_hbm, key_ref), (do_hbm, do_ref), (home_hbm, plan_ref))
    copies = [pltpu.make_async_copy(*pair, sems.at[i]) for i, pair in enumerate(pairs)]
    for copy in copies:
        copy.start()
    block = q_ref.shape[0]
    seg_own = own_ids(v_ref, block)
    seg_rows = jnp.broadcast_to(seg_own, (block, block))
    own_ok = triangle(block, 1) & (seg_rows == seg_rows.T)
    bias_ref[...] = jnp.where(own_ok, 0.0, NEG)
    joined_ref[...] = jnp.where(seg_rows == seg_own[:, 0:1], 0.0, NEG)
    for source, own_ref, turned, product, waits in (
        (q_ref, key_ref, qt_ref, s0_ref, copies[:2]),
        (do_ref, v_ref, gt_ref, gw0_ref, copies[2:]),
    ):
        for copy in waits:
            copy.wait()
        for g in range(qt_ref.shape[0]):
            turned[g] = stacked(source, g).T
            product[g] = dot(own_ref[0:block, g * HEAD_DIM : (g + 1) * HEAD_DIM], turned[g], NN)


def sent_kernel(q_ref, do_ref, gt_ref, gw0_ref, own_ref, far_ref, near_ref, p_ref, gs_ref, d2_ref, dk1_ref, dv1_ref):
    block = q_ref.shape[0]
    tri_g, lower = triangle(block, GROUP), lower_mask(block)
    scaling = 1.0 / math.sqrt(HEAD_DIM)
    def products(g):
        values = head_blocks(g, block, own_ref, far_ref, near_ref)
        return dot(jnp.concatenate(values[1:], axis=0), gt_ref[g], NN)

    heads = gt_ref.shape[0]
    upcoming = products(0)
    for g in range(heads):
        score_terms, upcoming = upcoming, products(g + 1) if g + 1 < heads else None
        queries, grads = stacked(q_ref, g), stacked(do_ref, g)
        w_xb = p_ref[g, 0:block]
        w_x = w_xb.astype(F32)
        w_n = p_ref[g, block : 2 * block]
        w_nf = w_n.astype(F32)
        gw_x = jnp.where(tri_g, gw0_ref[g], score_terms[block:])
        gw_n = score_terms[0:block]
        delta = jnp.sum(w_x * gw_x + w_nf * gw_n, axis=0, keepdims=True)
        gs_x = (w_x * (gw_x - delta)).astype(BF16)
        gs_n = (w_nf * (gw_n - delta)).astype(BF16)
        gs_ref[g, 0:block] = gs_x
        gs_ref[g, block : 2 * block] = gs_n
        _, gs_2 = split(lower, gs_x)
        _, w_2 = split(lower, w_xb)
        cols = slice(g * HEAD_DIM, (g + 1) * HEAD_DIM)
        dk = (dot(jnp.concatenate([gs_n, gs_2], axis=0), queries, NN) * scaling).astype(d2_ref.dtype)
        dv = dot(jnp.concatenate([w_n, w_2], axis=0), grads, NN).astype(d2_ref.dtype)
        dk1_ref[:, cols] = dk[0:block]
        dv1_ref[:, cols] = dv[0:block]
        d2_ref[0:block, cols] = dk[block:]
        d2_ref[block : 2 * block, cols] = dv[block:]


def kept_kernel(q_ref, do_ref, own_ref, far_ref, near_ref, p_ref, gs_ref, dq_ref, d0_ref, mark_ref):
    mark_ref[...] = jnp.zeros_like(mark_ref)
    block = q_ref.shape[0]
    lower = lower_mask(block)
    scaling = 1.0 / math.sqrt(HEAD_DIM)
    for g in range(own_ref.shape[1] // HEAD_DIM):
        keys = head_blocks(g, block, own_ref, far_ref, near_ref)
        queries, grads = stacked(q_ref, g), stacked(do_ref, g)
        gs_0, gs_2 = split(lower, gs_ref[g, 0:block])
        w_0, _ = split(lower, p_ref[g, 0:block])
        gs_n = gs_ref[g, block : 2 * block]
        cols = slice(g * HEAD_DIM, (g + 1) * HEAD_DIM)
        d0_ref[0:block, cols] = dot(gs_0, queries, NN) * scaling
        d0_ref[block : 2 * block, cols] = dot(w_0, grads, NN)
        dq = dot(jnp.concatenate([gs_0, gs_n, gs_2], axis=0), jnp.concatenate(keys, axis=0), TN)
        for h in range(GROUP):
            heads = slice((g * GROUP + h) * HEAD_DIM, (g * GROUP + h + 1) * HEAD_DIM)
            dq_ref[:, heads] = (dq[h * block : (h + 1) * block] * scaling).astype(dq_ref.dtype)


def bundle_kernel(seg_hbm, other_ref, v_hbm, own_ref, seg_ref, sems):
    block = v_hbm.shape[0]
    copies = [
        pltpu.make_async_copy(seg_hbm, seg_ref, sems.at[0]),
        pltpu.make_async_copy(v_hbm, own_ref.at[0:block], sems.at[1]),
    ]
    for copy in copies:
        copy.start()
    tail = slice(block, block + SEG_ROWS)
    own_ref[tail, 2 * block :] = jnp.zeros((SEG_ROWS, own_ref.shape[1] - 2 * block), BF16)
    first_core = lax.rem(lax.axis_index("ctx"), 2) == 0
    copies[0].wait()
    own_ids, other_ids = seg_ref[...].astype(F32), other_ref[...].astype(F32)
    ids = (jnp.where(first_core, own_ids, other_ids), jnp.where(first_core, other_ids, own_ids))
    for core in range(2):
        cols = slice(core * block, (core + 1) * block)
        own_ref[tail, cols] = jnp.broadcast_to(ids[core], (SEG_ROWS, block)).astype(BF16)
    copies[1].wait()


def pick_kernel(colours, own_ref, *rest):
    moved_refs, (_, out_ref, crossing_ref) = rest[:colours], rest[colours:]
    chip, core = lax.axis_index("ctx") // 2, lax.rem(lax.axis_index("ctx"), 2)
    colour = lax.rem(chip + colours - 1, colours)
    picked = moved_refs[0][...]
    for i in range(1, colours):
        picked = jnp.where(colour == colours - 1 - i, moved_refs[i][...], picked)
    out_ref[...] = picked
    block = min(own_ref.shape[0], crossing_ref.shape[0])
    crossing_ref[0:block] = jnp.where(core == 0, own_ref[0:block], picked[0:block])
    if crossing_ref.shape[0] > block:
        crossing_ref[block:] = jnp.zeros((crossing_ref.shape[0] - block, own_ref.shape[1]), BF16)


def merge_kernel(d2_ref, dk1_ref, dv1_ref, out_ref):
    block = dk1_ref.shape[0]
    odd = lax.rem(lax.axis_index("ctx"), 2) == 1
    for part, d1_ref in enumerate((dk1_ref, dv1_ref)):
        rows = slice(part * block, (part + 1) * block)
        other = jnp.where(odd, d1_ref[...].astype(F32), 0.0)
        out_ref[rows] = (d2_ref[rows].astype(F32) + other).astype(out_ref.dtype)


def source_row(row, step, count):
    return row ^ step if count & (count - 1) == 0 else lax.rem(row - step + count, count)


def early_kernel(n_dp, kept_ref, far_ref, own_ref, out_ref, sems):
    row = lax.axis_index("dp")
    copies = [
        pltpu.make_async_copy(own_ref, out_ref.at[0, 0, row], sems.at[0]),
        pltpu.make_async_copy(
            far_ref, out_ref.at[0, 0, source_row(row, n_dp - 1, n_dp)], sems.at[1]
        ),
    ]
    for copy in copies:
        copy.start()
    for copy in copies:
        copy.wait()


def finish_kernel(n_dp, n_ctx, *rest):
    pieces, rest = rest[: n_dp - 2], rest[n_dp - 2 :]
    uneven_ref, even_ref, dk1_ref, dv1_ref, d0_ref, _, out_ref, dk_ref, dv_ref, total_ref, sems = rest
    row, column = lax.axis_index("dp"), lax.axis_index("ctx")
    block = dk_ref.shape[0]
    copies = []
    for i in range(n_dp - 2):
        target = out_ref.at[0, 0, source_row(row, n_dp - 2 - i, n_dp)]
        copies.append(pltpu.make_async_copy(pieces[i], target, sems.at[i]))
        copies[-1].start()
    for part, (d1_ref, target) in enumerate(((dk1_ref, dk_ref), (dv1_ref, dv_ref))):
        rows = slice(part * block, (part + 1) * block)
        total = d0_ref[rows]
        total = total + jnp.where(lax.rem(column, 2) == 0, d1_ref[...].astype(F32), 0.0)
        d2 = jnp.where(lax.rem(column // 2, 2) == 0, even_ref[rows], uneven_ref[rows])
        total = total + jnp.where(column + 2 < n_ctx, d2.astype(F32), 0.0)
        total_ref[rows] = total.astype(total_ref.dtype)
        copies.append(pltpu.make_async_copy(total_ref.at[rows], target, sems.at[n_dp - 2 + part]))
        copies[-1].start()
    for copy in copies:
        copy.wait()


VMEM = pl.BlockSpec(memory_space=pltpu.VMEM)
HBM = pl.BlockSpec(memory_space=pl.ANY)


def params(kib=32 * 1024):
    return pltpu.CompilerParams(vmem_limit_bytes=kib * 1024)


def cost(flops, nbytes):
    return pl.CostEstimate(flops=flops, bytes_accessed=nbytes, transcendentals=0)


def pinned(*arrays):
    return [pltpu.with_memory_space_constraint(array, pltpu.HBM) for array in arrays]


def swap(value):
    count = lax.axis_size("ctx")
    return lax.ppermute(value, "ctx", [(i, i ^ 1) for i in range(count)])


def from_chip(value, colours):
    count = lax.axis_size("ctx")

    def pairs(colour):
        found = []
        for i in range(count):
            chip, core = i // 2, i % 2
            other = chip + 1 if chip % colours == colour else chip - 1 if (chip - 1) % colours == colour else -1
            found.append((i, 2 * other + core if 0 <= other < count // 2 else i ^ 1))
        return found

    return [lax.ppermute(value, "ctx", pairs(colour)) for colour in range(colours)]


def exchange(value, k):
    count = lax.axis_size("dp")
    if count & (count - 1) == 0:
        pairs = [(i, i ^ k) for i in range(count)]
    else:
        pairs = [(i, (i + k) % count) for i in range(count)]
    return lax.ppermute(value, "dp", pairs)


def on_device(query_rows, key_rows, value_rows, out_grad, segment_ids, home_rows):
    n_dp, n_ctx = lax.axis_size("dp"), lax.axis_size("ctx")
    query, grad = query_rows[0], out_grad[0]
    block, width = query.shape
    kv_width = key_rows.shape[2]
    heads = kv_width // HEAD_DIM
    pieces = home_rows.shape[1]
    capacity = max(2, 2 * pieces // n_dp)
    piece_len = block // pieces
    column = lax.axis_index("ctx")
    keys = key_rows[0]
    moved_keys = from_chip(keys, 3)
    values = pl.pallas_call(
        bundle_kernel,
        out_shape=jax.ShapeDtypeStruct((block + SEG_ROWS, kv_width), BF16),
        in_specs=[HBM, VMEM, HBM],
        out_specs=VMEM,
        scratch_shapes=[pltpu.VMEM((1, block), jnp.int32), pltpu.SemaphoreType.DMA((2,))],
        compiler_params=params(),
        cost_estimate=cost(0, 0),
        name="bundle",
    )(*pinned(segment_ids), swap(segment_ids), *pinned(value_rows[0]))
    moved_values = from_chip(values, 2)

    turned = jax.ShapeDtypeStruct((heads, HEAD_DIM, GROUP * block), BF16)
    product = jax.ShapeDtypeStruct((heads, block, GROUP * block), F32)
    plan, turned_query, turned_grad, own_scores, own_terms, query, grad, own_keys, *masks = pl.pallas_call(
        ahead_kernel,
        out_shape=[
            jax.ShapeDtypeStruct(home_rows.shape, jnp.int32), turned, turned, product, product,
            jax.ShapeDtypeStruct(query.shape, BF16), jax.ShapeDtypeStruct(grad.shape, BF16),
            jax.ShapeDtypeStruct(keys.shape, BF16),
            jax.ShapeDtypeStruct((block, block), F32), jax.ShapeDtypeStruct((block, block), F32),
        ],
        in_specs=[HBM] * 4 + [VMEM],
        out_specs=[VMEM] * 10,
        scratch_shapes=[pltpu.SemaphoreType.DMA((4,))],
        compiler_params=params(),
        cost_estimate=cost(0, 0),
        name="ahead",
    )(*pinned(home_rows, query, grad, keys), values)
    far_keys, crossing = pl.pallas_call(
        functools.partial(pick_kernel, len(moved_keys)),
        out_shape=[
            jax.ShapeDtypeStruct(keys.shape, BF16), jax.ShapeDtypeStruct(values.shape, BF16)
        ],
        in_specs=[VMEM] * (1 + len(moved_keys)) + [HBM],
        out_specs=[VMEM] * 2,
        compiler_params=params(),
        cost_estimate=cost(0, 0),
        name="pick_keys",
    )(own_keys, *moved_keys[::-1], plan)
    near_keys = swap(crossing)
    far_values, crossing = pl.pallas_call(
        functools.partial(pick_kernel, len(moved_values)),
        out_shape=[
            jax.ShapeDtypeStruct(values.shape, BF16), jax.ShapeDtypeStruct(keys.shape, BF16)
        ],
        in_specs=[VMEM] * (1 + len(moved_values)) + [HBM],
        out_specs=[VMEM] * 2,
        compiler_params=params(),
        cost_estimate=cost(0, 0),
        name="pick_values",
    )(values, *moved_values[::-1], plan)
    near_values = swap(crossing)
    weights = pl.pallas_call(
        weights_kernel,
        out_shape=jax.ShapeDtypeStruct((heads, 2 * block, GROUP * block), BF16),
        in_specs=[VMEM] * 9,
        out_specs=VMEM,
        compiler_params=params(),
        cost_estimate=cost(0, 0),
        name="weights",
    )(turned_query, own_scores, own_keys, far_keys, near_keys, values, far_values, *masks)
    sends = pl.pallas_call(
        functools.partial(attend_kernel, n_dp),
        out_shape=[jax.ShapeDtypeStruct((capacity, piece_len, width), BF16)] * n_dp,
        in_specs=[HBM] + [VMEM] * 4,
        out_specs=[VMEM] * n_dp,
        scratch_shapes=[
            pltpu.VMEM((pieces + 1, piece_len, width), BF16),
            pltpu.SMEM((n_dp,), jnp.int32),
            pltpu.SMEM((n_dp * capacity,), jnp.int32),
            pltpu.SMEM((1, pieces), jnp.int32),
            pltpu.SemaphoreType.DMA,
        ],
        compiler_params=params(),
        cost_estimate=cost(0, 0),
        name="attend",
    )(plan, weights, values, far_values, near_values)
    arrived = [exchange(sends[k], k) for k in range(n_dp - 1, 0, -1)] + [sends[0]]
    terms = jax.ShapeDtypeStruct((2 * block, kv_width), BF16)
    half = jax.ShapeDtypeStruct((block, kv_width), BF16)
    mark = jax.ShapeDtypeStruct((8, HEAD_DIM), F32)
    score_grads, d2, dk1, dv1 = pl.pallas_call(
        sent_kernel,
        out_shape=[jax.ShapeDtypeStruct(weights.shape, BF16), terms, half, half],
        in_specs=[VMEM] * 8,
        out_specs=[VMEM] * 4,
        compiler_params=params(),
        cost_estimate=cost(0, 0),
        name="sent_terms",
    )(query, grad, turned_grad, own_terms, values, far_values, near_values, weights)
    dq, d0, after_kept = pl.pallas_call(
        kept_kernel,
        out_shape=[
            jax.ShapeDtypeStruct((block, width), BF16),
            jax.ShapeDtypeStruct((2 * block, kv_width), F32),
            mark,
        ],
        in_specs=[VMEM] * 7,
        out_specs=[VMEM] * 3,
        compiler_params=params(),
        cost_estimate=cost(1073741824, 0),
        name="kept_terms",
    )(query, grad, own_keys, far_keys, near_keys, weights, score_grads)
    dk1_in, dv1_in = swap(dk1), swap(dv1)
    d2_sum = pl.pallas_call(
        merge_kernel,
        out_shape=terms,
        in_specs=[VMEM] * 3,
        out_specs=VMEM,
        compiler_params=params(),
        cost_estimate=cost(0, 0),
        name="merge",
    )(d2, dk1_in, dv1_in)
    d2_even, d2_uneven = from_chip(d2_sum, 2)
    routed_shape = jax.ShapeDtypeStruct((1, 1, n_dp, capacity, piece_len, width), BF16)
    routed = pl.pallas_call(
        functools.partial(early_kernel, n_dp),
        out_shape=routed_shape,
        in_specs=[HBM] * 3,
        out_specs=HBM,
        scratch_shapes=[pltpu.SemaphoreType.DMA((2,))],
        compiler_params=params(),
        cost_estimate=cost(2147483648, 0),
        name="place_early",
    )(after_kept, arrived[0], arrived[-1])
    routed, dk, dv = pl.pallas_call(
        functools.partial(finish_kernel, n_dp, n_ctx),
        out_shape=[routed_shape] + [jax.ShapeDtypeStruct((block, kv_width), BF16)] * 2,
        in_specs=[HBM] * (n_dp - 2) + [VMEM] * 5 + [HBM],
        out_specs=[HBM] * 3,
        input_output_aliases={n_dp + 3: 0},
        scratch_shapes=[
            pltpu.VMEM((2 * block, kv_width), BF16),
            pltpu.SemaphoreType.DMA((n_dp,)),
        ],
        compiler_params=params(),
        cost_estimate=cost(0, 1 << 20),
        name="finish",
    )(*arrived[1:-1], d2_uneven, d2_even, dk1_in, dv1_in, d0, *pinned(routed))
    return routed, dq[None], dk[None], dv[None]


def solution(mesh):
    rows = P("dp", "ctx", None)
    return jax.shard_map(
        on_device,
        mesh=mesh,
        in_specs=(rows, rows, rows, rows, P("dp", "ctx"), P("dp", "ctx")),
        out_specs=(P("dp", "ctx", None, None, None, None), rows, rows, rows),
        check_vma=False,
    )
```
